512 devices in a mesh: ctx: 16 (over z), exp: 32 (over y, x, core).
Axes of the slice: x: 4, y: 4, z: 16, core: 2. Of those that a mesh axis runs over, the one named last changes fastest.
Arguments:
- queries: bfloat16 [16384, 4096], P('ctx', 'exp'), may hold values from -6 to 6
- key_vectors: bfloat16 [16384, 4096], P('ctx', 'exp'), may hold values from -6 to 6
- value_vectors: bfloat16 [16384, 4096], P('ctx', 'exp'), may hold values from -6 to 6
- log_decay: float32 [16384, 32], P('ctx', 'exp'), may hold values from -2 to 0
- attn_gain: float32 [4096], P('exp'), may hold values from 0.1 to 1.9
- residual: bfloat16 [16384, 4096], P(('ctx', 'exp')), may hold values from -6 to 6
- expert_ids: int32 [16384, 1], P(('ctx', 'exp')), may hold values from 0 to 31; in each aligned block of 32 rows (0 to 31, 32 to 63, ...) at most 2 rows name the same one
- gate_weights: float32 [16384, 1], P(('ctx', 'exp')), may hold values from 0.5 to 1.5
- w_gate: bfloat16 [32, 4096, 768], P('exp', 'ctx'), may hold values from -0.09375 to 0.09375
- w_up: bfloat16 [32, 4096, 768], P('exp', 'ctx'), may hold values from -0.09375 to 0.09375
- w_down: bfloat16 [32, 768, 4096], P('exp', None, 'ctx'), may hold values from -0.21875 to 0.21875
Outputs:
- mixed: bfloat16 [16384, 4096], P(('ctx', 'exp'))
The draws below stay inside these ranges and needn't reach their ends.
Inputs may be any that keep to these rules, and one draw needn't show every extreme that they name: `expert_ids`: within the rows of one device (aligned blocks of 32 rows) no expert is named more than 2 times.
All inputs are finite; a program needn't handle non-finite values.
Results may differ from the reference program's by a relative error of at most 0.03.
Values may be sent and summed in bfloat16 or wider, within the bound.
A program may use at most 64 MiB of HBM per device.

```python
import math
import jax
import jax.numpy as jnp
import numpy as np
from jax import lax

HD = 128
HEADS = 32
D = 4096
FFE = 768
EXPERTS = 32
TOP = 1
SEC = 1024
SEQ = 16384
BL = 512
ROWS = 32
CAP = 2
DS = 256
N_CTX = 16
N_EXP = 32


def draw_log_decay(key, part):
    key = jax.random.fold_in(key, 7)
    keys = jax.random.split(key, 7)
    share = 0.5
    slow_heads = jax.random.uniform(keys[0], (HEADS,)) < share
    chain_loss = jnp.exp(jax.random.uniform(keys[1], (HEADS,), minval=jnp.log(0.22), maxval=jnp.log(0.9)))
    slow_rate = chain_loss / SEQ
    fast_rate = jnp.exp(jax.random.uniform(keys[2], (HEADS,), minval=jnp.log(1.0 / 50.0), maxval=jnp.log(1.0 / 30.0)))
    baseline_decay_rate = jnp.where(slow_heads, slow_rate, fast_rate)
    jitter_level = jnp.exp(jax.random.uniform(keys[3], (SEQ, HEADS), minval=-0.7, maxval=0.7))
    section_factor = jnp.exp(jax.random.uniform(keys[4], (SEQ // SEC, HEADS), minval=-0.7, maxval=0.7))
    local_variation = jnp.repeat(section_factor, SEC, axis=0)
    marked_locations = jax.random.randint(keys[5], (2, HEADS), 0, SEQ)
    retained_fraction = jax.random.uniform(keys[6], (2, HEADS), minval=0.5, maxval=0.8)
    position_lookup = jnp.arange(SEQ)[:, None]
    spike_events = jnp.where(position_lookup == marked_locations[0][None, :], jnp.log(retained_fraction[0])[None, :], 0.0)
    spike_events = spike_events + jnp.where(position_lookup == marked_locations[1][None, :], jnp.log(retained_fraction[1])[None, :], 0.0)
    return (-baseline_decay_rate[None, :] * jitter_level * local_variation + spike_events).astype(jnp.float32)


def level_of(stream_key, shape, cuts, least, top_value):
    gain, own = 1.0, jax.random.fold_in(stream_key, 6)
    for dim, shards_of in cuts:
        steps = jnp.exp(jax.random.uniform(jax.random.fold_in(own, dim), (shards_of,), jnp.float32, least / len(cuts), top_value / len(cuts)))
        gain = gain * jnp.repeat(steps, shape[dim] // shards_of).reshape([-1 if axis == dim else 1 for axis in range(len(shape))])
    return gain


def routed_block(key, own, number, rows, amount, top, limit, lean):
    sequence = jax.random.permutation(key, amount)
    crowded, ordinary = shares(amount, rows * top, limit, lean, True), shares(amount, rows * top, limit, lean, False)
    places = jnp.arange(amount)

    def named(lengths, offset_by):
        used = int((lengths > 0).sum())
        fixed = max(1, used // 4)
        passed = fixed + (places - fixed + offset_by * (used - fixed)) % max(1, amount - fixed)
        return jnp.zeros((amount,), jnp.int32).at[sequence[jnp.where(places < fixed, places, passed)]].set(jnp.asarray(lengths, jnp.int32))

    lengths = jnp.where(number % 4 == 0, named(crowded, number // 4), named(ordinary, number - number // 4 - 1))
    mixed = jax.random.permutation(jax.random.fold_in(own, 3), amount)
    donor, sink = mixed[0:amount // 2 * 2:2], mixed[1:amount // 2 * 2:2]
    slack = jnp.minimum(lengths[donor] - 1, limit - lengths[sink]) // 2
    slack = jnp.where((donor == sequence[0]) | (sink == sequence[0]) | (lengths[sink] == 0), 0, jnp.maximum(slack, 0))
    passed = jax.random.randint(jax.random.fold_in(own, 4), (amount // 2,), 0, 1 << 20) % (slack + 1)
    lengths = lengths.at[donor].add(-passed).at[sink].add(passed)
    members = jnp.searchsorted(jnp.cumsum(lengths), jnp.arange(rows * top), side="right").astype(jnp.int32)
    table = members.reshape(top, rows).T
    table = table[jax.random.permutation(jax.random.fold_in(own, 1), rows)]
    offset_by = jax.random.randint(jax.random.fold_in(own, 2), (rows, 1), 0, top)
    return jnp.take_along_axis(table, (jnp.arange(top)[None, :] + offset_by) % top, axis=1)


def shares(count, total, limit, lean, full):
    weights = [(1 << 20) // math.isqrt(standing ** lean) + 1 for standing in range(1, count + 1)]
    largest = limit if full else min(limit, max(-(-total // count), total * weights[0] // sum(weights)))
    least = 1 if total - largest >= count - 1 else 0
    holding, surplus = [largest] + [least] * (count - 1), total - largest - least * (count - 1)
    while surplus > 0:
        candidates = [i for i in range(1, count) if holding[i] < largest] or [i for i in range(1, count) if holding[i] < limit]
        whole, remaining = sum([weights[i] for i in candidates]), surplus
        for i in candidates:
            addition = min(limit - holding[i], max(1, remaining * weights[i] // whole), surplus)
            holding[i] = holding[i] + addition
            surplus = surplus - addition
    return np.array(holding)


def centred(own_key, extent, scale, reach, shards=(), dtype=jnp.bfloat16):
    level = level_of(own_key, extent, shards, -0.22, 0.18) if shards else 1.0
    values = jax.random.normal(own_key, extent, jnp.float32) * scale * level
    return jnp.minimum(jnp.maximum(values, -reach), reach).astype(dtype)


def setup_inputs(seed: int = 0) -> dict:
    arg_keys = jax.random.split(jax.random.key(seed), 12)
    queries = centred(arg_keys[0], (SEQ, D), 1.0, 6.0, ((0, 16), (1, 32)))
    key_vectors = centred(arg_keys[1], (SEQ, D), 1.0, 6.0, ((0, 16), (1, 32)))
    value_vectors = centred(arg_keys[2], (SEQ, D), 1.0, 6.0, ((0, 16), (1, 32)))
    log_decay = draw_log_decay(jax.random.fold_in(arg_keys[11], 71), 0)
    attn_gain = jnp.clip(1.0 + 0.18 * jax.random.normal(arg_keys[4], (D,), jnp.float32), 0.1, 1.9)
    residual = centred(arg_keys[5], (SEQ, D), 1.0, 6.0, ((0, 512),))
    expert_ids_keys = jax.random.split(jax.random.fold_in(arg_keys[6], 1), SEQ // ROWS)
    expert_ids_turns = jax.random.permutation(jax.random.fold_in(arg_keys[6], 3), SEQ // ROWS)
    expert_ids = jax.vmap(lambda own, number: routed_block(jax.random.fold_in(arg_keys[6], 2), own, number, ROWS, EXPERTS, TOP, CAP, 2))(expert_ids_keys, expert_ids_turns).reshape((SEQ, TOP))
    gate_weights = jnp.clip(0.5 + 1.0 * jax.random.uniform(arg_keys[7], (SEQ, TOP), jnp.float32) ** level_of(arg_keys[7], (SEQ, TOP), ((0, 512),), -0.2, 0.2), 0.5, 1.5)
    w_gate = centred(arg_keys[8], (EXPERTS, D, FFE), D ** -0.5, 0.09375, ((0, 32), (1, 16)))
    w_up = centred(arg_keys[9], (EXPERTS, D, FFE), D ** -0.5, 0.09375, ((0, 32), (1, 16)))
    w_down = centred(arg_keys[10], (EXPERTS, FFE, D), FFE ** -0.5, 0.21875, ((0, 32), (2, 16)))
    return {"queries": queries, "key_vectors": key_vectors, "value_vectors": value_vectors, "log_decay": log_decay, "attn_gain": attn_gain, "residual": residual, "expert_ids": expert_ids, "gate_weights": gate_weights, "w_gate": w_gate, "w_up": w_up, "w_down": w_down}


PRECISE = lax.Precision.HIGHEST
EPSILON = 1e-06

def head_attention(inputs):
    query_rows, key_rows, value_rows, decay_rows = inputs
    blocks = query_rows.shape[0] // BL
    query_blocks = query_rows.reshape(blocks, BL, HD).astype(jnp.float32)
    key_blocks = key_rows.reshape(blocks, BL, HD).astype(jnp.float32)
    value_blocks = value_rows.reshape(blocks, BL, HD)
    decay_blocks = decay_rows.reshape(blocks, BL)
    causal = jnp.arange(BL)[:, None] >= jnp.arange(BL)[None, :]

    def advance(carried, current):
        query_block, key_block, value_block, decay_block = current
        running = jnp.cumsum(decay_block)
        ending = running[-1]
        scores = jnp.dot(query_block, key_block.T, precision=PRECISE)
        spread = jnp.where(causal, running[:, None] - running[None, :], -jnp.inf)
        weights = (scores * jnp.exp(spread)).astype(jnp.bfloat16)
        within = jnp.dot(weights, value_block, preferred_element_type=jnp.float32)
        query_decayed = query_block * jnp.exp(running)[:, None]
        across = jnp.dot(query_decayed, carried, precision=PRECISE)
        key_decayed = key_block * jnp.exp(ending - running)[:, None]
        update = jnp.dot(key_decayed.T, value_block.astype(jnp.float32), precision=PRECISE)
        carried = jnp.exp(ending) * carried + update
        return (carried, within + across)
    start_state = jnp.zeros((HD, HD), jnp.float32)
    _, output = lax.scan(advance, start_state, (query_blocks, key_blocks, value_blocks, decay_blocks))
    return output.reshape(blocks * BL, HD)

def reference(queries, key_vectors, value_vectors, log_decay, attn_gain, residual, expert_ids, gate_weights, w_gate, w_up, w_down):

    def by_head(stacked):
        return stacked.reshape(SEQ, HEADS, HD).transpose(1, 0, 2)
    attention = lax.map(head_attention, (by_head(queries), by_head(key_vectors), by_head(value_vectors), log_decay.T))
    inverse_rms = lax.rsqrt(lax.optimization_barrier(jnp.mean(attention * attention, axis=-1, keepdims=True)) + EPSILON)
    normed = (attention * inverse_rms * attn_gain.reshape(HEADS, 1, HD)).astype(jnp.bfloat16)
    normed = normed.transpose(1, 0, 2).reshape(SEQ, D)
    hidden_in = (residual.astype(jnp.float32) + normed.astype(jnp.float32)).astype(jnp.bfloat16)
    chosen = expert_ids[:, 0]
    most_rows = N_CTX * N_EXP * CAP
    pieces = D // DS

    def run_expert(expert):
        matches = chosen == expert
        picked = jnp.nonzero(matches, size=most_rows, fill_value=0)[0].astype(jnp.int32)
        how_many = jnp.sum(matches.astype(jnp.int32))
        taken_rows = hidden_in[picked].astype(jnp.float32).reshape(most_rows, pieces, DS)
        gate_mat = w_gate[expert].astype(jnp.float32).reshape(pieces, DS, FFE)
        up_mat = w_up[expert].astype(jnp.float32).reshape(pieces, DS, FFE)
        gate_parts = jnp.einsum('rcd,cdf->crf', taken_rows, gate_mat, precision=PRECISE)
        up_parts = jnp.einsum('rcd,cdf->crf', taken_rows, up_mat, precision=PRECISE)
        gate_sum = lax.optimization_barrier(jnp.sum(lax.optimization_barrier(gate_parts.astype(jnp.bfloat16)).astype(jnp.float32), axis=0))
        up_sum = lax.optimization_barrier(jnp.sum(lax.optimization_barrier(up_parts.astype(jnp.bfloat16)).astype(jnp.float32), axis=0))
        activated = (jax.nn.silu(gate_sum) * up_sum).astype(jnp.bfloat16)
        produced = jnp.dot(activated, w_down[expert], preferred_element_type=jnp.float32).astype(jnp.bfloat16)
        is_valid = jnp.arange(most_rows) < how_many
        return (picked, jnp.where(is_valid[:, None], produced.astype(jnp.float32), 0.0))

    def accumulate(running_sum, expert):
        picked, produced = run_expert(expert)
        return (running_sum.at[picked].add(produced), None)
    combined, _ = lax.scan(accumulate, jnp.zeros((SEQ, D), jnp.float32), jnp.arange(EXPERTS).astype(jnp.int32))
    mixed = hidden_in.astype(jnp.float32) + gate_weights[:, 0:1] * combined
    return mixed.astype(jnp.bfloat16)
```

```python
import functools

import jax
import jax.numpy as jnp
from jax import lax
from jax.experimental import pallas as pl
from jax.experimental.pallas import tpu as pltpu
from jax.sharding import PartitionSpec as P

MESH = pl.DeviceIdType.MESH
F32, BF16 = jnp.float32, jnp.bfloat16
PRECISE = lax.Precision.HIGHEST
EPSILON = 1e-06
NZ, NE = 16, 32
HD, BL, SEC, ROWS, DS, FFE = 128, 512, 1024, 32, 256, 768
TILES = SEC // 128
CHUNK = 64
HALF = NZ // 2
SUBS = 4
WIDE = 2 * FFE // SUBS


def dot(a, b, **kw):
    return jnp.dot(a, b, preferred_element_type=F32, **kw)


def dot_t(a, b):
    return lax.dot_general(a, b, (((1,), (1,)), ((), ())), preferred_element_type=F32)


def t_dot(a, b):
    return lax.dot_general(a, b, (((0,), (0,)), ((), ())), preferred_element_type=F32)


def iota(shape, dim):
    return lax.broadcasted_iota(jnp.int32, shape, dim)


def kernel(
    q_ref, k_ref, v_ref, decay_ref, gain_ref, res_ref, ids_ref, gw_ref, wg_ref, wu_ref, wd_ref,
    out_ref,
    info, coef, group, quarter, prefix, within, normed, heads, hidden, zrows, place, slots, erows,
    send_r, recv_r, send_l, recv_l, act, produced, fromexp, yrows, yback,
    s_info, r_info, s_grp, r_grp, s_qtr, r_qtr, s_pre, r_pre, s_hd, r_hd, s_zr, r_zr, s_sl, r_sl,
    s_rr, r_rr, s_rl, r_rl, s_ar, r_ar, s_al, r_al, s_pr, r_pr, s_yb, r_yb,
):
    z, e = lax.axis_index("ctx"), lax.axis_index("exp")
    right, left = lax.rem(z + 1, NZ), lax.rem(z + NZ - 1, NZ)
    member, base = lax.rem(z, 4), z - lax.rem(z, 4)
    grp = z // 4

    def remote(src, dst, ss, rs, to_z, to_e):
        return pltpu.make_async_remote_copy(
            src_ref=src, dst_ref=dst, send_sem=ss, recv_sem=rs,
            device_id=(to_z, to_e), device_id_type=MESH,
        )

    def loop(lo, hi, body):
        def step(i, c):
            body(i)
            return c
        lax.fori_loop(lo, hi, step, 0)

    barrier = pltpu.get_barrier_semaphore()
    loop(1, NZ, lambda i: pl.semaphore_signal(
        barrier, inc=1, device_id=(lax.rem(z + i, NZ), e), device_id_type=MESH))
    loop(1, NE, lambda i: pl.semaphore_signal(
        barrier, inc=1, device_id=(z, lax.rem(e + i, NE)), device_id_type=MESH))

    lane, sub = iota((ROWS, 128), 1), iota((ROWS, 128), 0)
    eye = iota((ROWS, ROWS), 1) == iota((ROWS, ROWS), 0)
    ids_col = jnp.sum(jnp.where(eye, ids_ref[...].astype(F32), 0.0), axis=1, keepdims=True)
    near = lax.rem(lane, ROWS)
    ids_row = jnp.sum(jnp.where(sub == near, ids_col, 0.0), axis=0, keepdims=True)
    same = jnp.where((ids_col == ids_row) & (sub < near), 1.0, 0.0)
    slot_row = ids_row * 32.0 + jnp.sum(same, axis=0, keepdims=True)

    decay = jnp.concatenate([decay_ref[:, 128 * r:128 * r + 128] for r in range(TILES)], axis=0)
    upto = jnp.where(iota((128, 128), 0) <= iota((128, 128), 1), 1.0, 0.0)
    cum = dot(decay, upto, precision=PRECISE)
    tail = jnp.broadcast_to(cum[:, 127:128], (TILES, 128))
    r_to, r_from = iota((TILES, TILES), 0), iota((TILES, TILES), 1)
    earlier = jnp.where((r_from < r_to) & (r_from // 4 == r_to // 4), 1.0, 0.0)
    running = cum + dot(earlier, tail, precision=PRECISE)
    running_col = running.T
    ends = [running[4 * b + 3:4 * b + 4, 127:128] for b in range(2)]
    total = ends[0] + ends[1]

    updates = []
    for b in range(2):
        rest = jnp.concatenate(
            [jnp.exp(ends[b] - running_col[:, 4 * b + r:4 * b + r + 1]) for r in range(4)], axis=0
        )
        decayed = (v_ref[BL * b:BL * b + BL, :].astype(F32) * rest).astype(BF16)
        updates.append(t_dot(k_ref[BL * b:BL * b + BL, :], decayed))
    own_state = jnp.exp(ends[1]) * updates[0] + updates[1]

    quart = iota((1, 128), 1) // 32
    info[z] = jnp.where(quart == member, slot_row, 0.0) + jnp.where(
        quart == lax.rem(z + 1, 4), total, 0.0
    )
    group[member] = own_state.astype(BF16)
    pl.semaphore_wait(barrier, NZ - 1 + NE - 1)

    def cp_info(i):
        return remote(info.at[z], info.at[z], s_info.at[i], r_info.at[i], lax.rem(z + i, NZ), e)

    def cp_group(i):
        return remote(group.at[member], group.at[member], s_grp.at[i], r_grp.at[i],
                      base + lax.rem(member + i, 4), e)

    def cp_quarter(i):
        return remote(quarter.at[grp], quarter.at[grp], s_qtr.at[i], r_qtr.at[i],
                      lax.rem(z + 4 * i, NZ), e)

    def cp_prefix(i):
        return remote(prefix.at[member], prefix.at[member], s_pre.at[i], r_pre.at[i],
                      base + lax.rem(member + i, 4), e)

    loop(1, NZ, lambda i: cp_info(i).start())
    loop(1, 4, lambda i: cp_group(i).start())

    for b in range(2):
        for i in range(4):
            r, width = 4 * b + i, 128 * (i + 1)
            rows = pl.ds(128 * r, 128)
            span = pl.ds(BL * b, width)
            scores = dot_t(q_ref[rows, :], k_ref[span, :])
            col = running_col[:, r:r + 1]
            weights = []
            for j in range(i + 1):
                spread = col - running[4 * b + j:4 * b + j + 1, :]
                if j == i:
                    spread = jnp.where(iota((128, 128), 0) >= iota((128, 128), 1), spread, -jnp.inf)
                weights.append((scores[:, 128 * j:128 * j + 128] * jnp.exp(spread)).astype(BF16))
            weights = jnp.concatenate(weights, axis=1) if i else weights[0]
            within[rows, :] = dot(weights, v_ref[span, :])

    loop(1, NZ, lambda i: cp_info(i).wait_recv())
    table = info[:, 0, :]
    zrow, zlane = iota((NZ, 128), 0), iota((NZ, 128), 1)
    totals = jnp.sum(jnp.where(zlane == 32 * lax.rem(zrow + 1, 4), table, 0.0), axis=1, keepdims=True)
    totals = jnp.broadcast_to(totals, (NZ, 128))
    src, mid = iota((NZ, NZ), 0), iota((NZ, NZ), 1)

    def decays(mask, keep):
        between = dot(jnp.where(mask, 1.0, 0.0), totals, precision=PRECISE)
        return jnp.where(keep, jnp.exp(between), 0.0)

    coef[0] = decays((mid > src) & (mid < base + 4), zrow >= 0)
    coef[1] = decays((mid >= 4 * src + 4) & (mid < base), zrow < grp)
    coef[2] = decays((mid > src) & (mid < z), zrow < z)
    coef[3] = decays((mid >= base) & (mid < z), zrow >= 0)

    loop(1, 4, lambda i: cp_group(i).wait_recv())
    part = pl.ds(pl.multiple_of(member * 32, 32), 32)
    whole = jnp.zeros((32, HD), F32)
    for m in range(4):
        whole += coef[0, pl.ds(base + m, 1), :] * group[m, part, :].astype(F32)
    quarter[grp] = whole.astype(BF16)
    loop(1, 4, lambda i: cp_quarter(i).start())
    loop(1, 4, lambda i: cp_quarter(i).wait_recv())
    before = jnp.zeros((32, HD), F32)
    for m in range(4):
        before += coef[1, m:m + 1, :] * quarter[m].astype(F32)
    prefix[member] = before.astype(BF16)
    loop(1, 4, lambda i: cp_prefix(i).start())
    incoming = jnp.zeros((HD, HD), F32)
    for m in range(4):
        incoming += coef[2, pl.ds(base + m, 1), :] * group[m].astype(F32)
    loop(1, 4, lambda i: cp_prefix(i).wait_recv())
    incoming += coef[3, 0:1, :] * prefix[...].reshape(HD, HD).astype(F32)

    gain = gain_ref[...]
    for b in range(2):
        state = incoming if b == 0 else updates[0] + jnp.exp(ends[0]) * incoming
        state = state.astype(BF16)
        for i in range(4):
            r = 4 * b + i
            rows = pl.ds(128 * r, 128)
            across = dot(q_ref[rows, :], state) * jnp.exp(running_col[:, r:r + 1])
            attention = within[rows, :] + across
            scale = lax.rsqrt(jnp.mean(attention * attention, axis=1, keepdims=True) + EPSILON)
            normed[rows, :] = (attention * scale * gain).astype(BF16)

    def cp_heads(i):
        to = lax.rem(e + i, NE)
        return remote(normed.at[pl.ds(pl.multiple_of(to * ROWS, ROWS), ROWS)], heads.at[e],
                      s_hd.at[i], r_hd.at[i], z, to)

    loop(1, NE, lambda i: cp_heads(i).start())
    heads[e] = normed[pl.ds(pl.multiple_of(e * ROWS, ROWS), ROWS), :]

    picks = []
    for g in range(4):
        mine = (zlane // 32 == lax.rem(zrow, 4)) & (zrow // 4 == g)
        row = jnp.sum(jnp.where(mine, table + 2.0 * zrow.astype(F32), 0.0), axis=0, keepdims=True)
        picks.append(row)
    picks = jnp.concatenate(picks, axis=1).astype(jnp.int32)
    for t in range(8):
        place[128 * t:128 * t + 128, :] = jnp.where(
            iota((128, NZ * ROWS), 0) + 128 * t == picks, 1.0, 0.0
        ).astype(BF16)

    loop(1, NE, lambda i: cp_heads(i).wait_recv())
    for c in range(NZ):
        both = jnp.concatenate([heads[2 * c], heads[2 * c + 1]], axis=1).astype(F32)
        hidden[c] = (res_ref[:, DS * c:DS * c + DS].astype(F32) + both).astype(BF16)

    def cp_rows(i):
        to = lax.rem(z + i, NZ)
        return remote(hidden.at[to], zrows.at[z], s_zr.at[i], r_zr.at[i], to, e)

    loop(1, NZ, lambda i: cp_rows(i).start())
    zrows[z] = hidden[z]
    loop(1, NZ, lambda i: cp_rows(i).wait_recv())
    slots[...] = dot(place[...], zrows[...].reshape(NZ * ROWS, DS)).astype(BF16)

    def cp_slots(i):
        to = lax.rem(e + i, NE)
        return remote(slots.at[pl.ds(pl.multiple_of(to * 32, 32), 32)], erows.at[e],
                      s_sl.at[i], r_sl.at[i], z, to)

    loop(1, NE, lambda i: cp_slots(i).start())
    erows[e] = slots[pl.ds(pl.multiple_of(e * 32, 32), 32), :]
    loop(1, NE, lambda i: cp_slots(i).wait_recv())

    def columns(u):
        side, off = divmod(u * WIDE, FFE)
        return (wg_ref, wu_ref)[side][:, off:off + WIDE]

    def own(dest, u):
        rows = erows[pl.ds(2 * dest, 2)].reshape(CHUNK, DS)
        return dot(rows, columns(u))

    def cp_right(s, u):
        return remote(send_r.at[s, u], recv_r.at[s, u], s_rr.at[s, u], r_rr.at[s, u], right, e)

    def cp_left(s, u):
        return remote(send_l.at[s, u], recv_l.at[s, u], s_rl.at[s, u], r_rl.at[s, u], left, e)

    for s in range(HALF):
        to_r = lax.rem(z + HALF - s, NZ)
        to_l = lax.rem(z + HALF + 1 + s, NZ)
        for u in range(SUBS):
            mine = own(to_r, u)
            if s:
                cp_right(s - 1, u).wait_recv()
                mine += recv_r[s - 1, u].astype(F32)
            send_r[s, u] = mine.astype(BF16)
            cp_right(s, u).start()
            if s < HALF - 1:
                mine = own(to_l, u)
                if s:
                    cp_left(s - 1, u).wait_recv()
                    mine += recv_l[s - 1, u].astype(F32)
                send_l[s, u] = mine.astype(BF16)
                cp_left(s, u).start()
    sums = []
    for u in range(SUBS):
        mine = own(z, u)
        cp_left(HALF - 2, u).wait_recv()
        mine += recv_l[HALF - 2, u].astype(F32)
        cp_right(HALF - 1, u).wait_recv()
        sums.append(mine + recv_r[HALF - 1, u].astype(F32))
    for u in range(SUBS // 2):
        gate, up = sums[u], sums[u + SUBS // 2]
        act[z, :, WIDE * u:WIDE * u + WIDE] = (gate / (1.0 + jnp.exp(-gate)) * up).astype(BF16)

    def cp_act_r(s, u):
        at = act.at[lax.rem(z + NZ - s, NZ), pl.ds(32 * u, 32)]
        return remote(at, at, s_ar.at[s, u], r_ar.at[s, u], right, e)

    def cp_act_l(s, u):
        at = act.at[lax.rem(z + s, NZ), pl.ds(32 * u, 32)]
        return remote(at, at, s_al.at[s, u], r_al.at[s, u], left, e)

    def cp_produced(d):
        return remote(produced.at[d], fromexp.at[e], s_pr.at[d], r_pr.at[e], z, d)

    def down(chunk):
        rows = dot(act[chunk], wd_ref[...]).astype(BF16)
        for u in range(2):
            d = 2 * chunk + u
            produced[d] = rows[32 * u:32 * u + 32]

            @pl.when(d != e)
            def _():
                cp_produced(d).start()

            @pl.when(d == e)
            def _():
                fromexp[e] = produced[d]

    for u in range(2):
        cp_act_r(0, u).start()
        cp_act_l(0, u).start()
    down(z)
    for s in range(HALF):
        for u in range(2):
            cp_act_r(s, u).wait_recv()
            if s < HALF - 1:
                cp_act_r(s + 1, u).start()
            if s < HALF - 1:
                cp_act_l(s, u).wait_recv()
                if s < HALF - 2:
                    cp_act_l(s + 1, u).start()
        down(lax.rem(z + NZ - 1 - s, NZ))
        if s < HALF - 1:
            down(lax.rem(z + 1 + s, NZ))

    def cp_from(i):
        src_e = lax.rem(e + i, NE)
        return remote(produced.at[src_e], fromexp.at[src_e], s_pr.at[src_e], r_pr.at[src_e], z, src_e)

    loop(1, NE, lambda i: cp_from(i).wait_recv())
    back = t_dot(place[...], fromexp[...].reshape(NE * 32, DS)).astype(BF16)
    yrows[...] = back.reshape(NZ, ROWS, DS)

    def cp_back(i):
        to = lax.rem(z + i, NZ)
        return remote(yrows.at[to], yback.at[z], s_yb.at[i], r_yb.at[i], to, e)

    loop(1, NZ, lambda i: cp_back(i).start())
    yback[z] = yrows[z]
    gw_col = jnp.sum(jnp.where(eye, gw_ref[...], 0.0), axis=1, keepdims=True)
    loop(1, NZ, lambda i: cp_back(i).wait_recv())
    for c in range(NZ):
        mixed = hidden[c].astype(F32) + gw_col * yback[c].astype(F32)
        out_ref[:, DS * c:DS * c + DS] = mixed.astype(BF16)

    loop(1, NZ, lambda i: cp_info(i).wait_send())
    loop(1, 4, lambda i: cp_group(i).wait_send())
    loop(1, 4, lambda i: cp_quarter(i).wait_send())
    loop(1, 4, lambda i: cp_prefix(i).wait_send())
    loop(1, NE, lambda i: cp_heads(i).wait_send())
    loop(1, NZ, lambda i: cp_rows(i).wait_send())
    loop(1, NE, lambda i: cp_slots(i).wait_send())
    for u in range(SUBS):
        for s in range(HALF):
            cp_right(s, u).wait_send()
            if s < HALF - 1:
                cp_left(s, u).wait_send()
    for u in range(2):
        for s in range(HALF):
            cp_act_r(s, u).wait_send()
            if s < HALF - 1:
                cp_act_l(s, u).wait_send()
    loop(1, NE, lambda i: cp_from(i).wait_send())
    loop(1, NZ, lambda i: cp_back(i).wait_send())


def shards(q, k, v, log_decay, gain, residual, ids, gate_weights, w_gate, w_up, w_down):
    sem = pltpu.SemaphoreType.DMA
    pair = lambda *shape: [sem(shape), sem(shape)]
    scratch = [
        pltpu.VMEM((NZ, 1, 128), F32),
        pltpu.VMEM((4, NZ, 128), F32),
        pltpu.VMEM((4, HD, HD), BF16),
        pltpu.VMEM((4, 32, HD), BF16),
        pltpu.VMEM((4, 32, HD), BF16),
        pltpu.VMEM((SEC, HD), F32),
        pltpu.VMEM((SEC, HD), BF16),
        pltpu.VMEM((NE, ROWS, HD), BF16),
        pltpu.VMEM((NZ, ROWS, DS), BF16),
        pltpu.VMEM((NZ, ROWS, DS), BF16),
        pltpu.VMEM((NE * 32, NZ * ROWS), BF16),
        pltpu.VMEM((NE * 32, DS), BF16),
        pltpu.VMEM((NE, 32, DS), BF16),
        pltpu.VMEM((HALF, SUBS, CHUNK, WIDE), BF16),
        pltpu.VMEM((HALF, SUBS, CHUNK, WIDE), BF16),
        pltpu.VMEM((HALF, SUBS, CHUNK, WIDE), BF16),
        pltpu.VMEM((HALF, SUBS, CHUNK, WIDE), BF16),
        pltpu.VMEM((NZ, CHUNK, FFE), BF16),
        pltpu.VMEM((NE, 32, DS), BF16),
        pltpu.VMEM((NE, 32, DS), BF16),
        pltpu.VMEM((NZ, ROWS, DS), BF16),
        pltpu.VMEM((NZ, ROWS, DS), BF16),
        *pair(NZ), *pair(4), *pair(4), *pair(4), *pair(NE), *pair(NZ), *pair(NE),
        *pair(HALF, SUBS), *pair(HALF, SUBS), *pair(HALF, 2), *pair(HALF, 2), *pair(NE), *pair(NZ),
    ]
    vmem = pl.BlockSpec(memory_space=pltpu.VMEM)
    return pl.pallas_call(
        kernel,
        out_shape=jax.ShapeDtypeStruct(residual.shape, BF16),
        in_specs=[vmem] * 11,
        out_specs=vmem,
        scratch_shapes=scratch,
        name="layer_pair",
        compiler_params=pltpu.CompilerParams(
            collective_id=0, has_side_effects=True, vmem_limit_bytes=48 << 20
        ),
    )(
        q, k, v, log_decay.T, gain.reshape(1, HD), residual, ids.T, gate_weights.T,
        w_gate[0], w_up[0], w_down[0],
    )


def solution(mesh):
    return jax.shard_map(
        shards,
        mesh=mesh,
        in_specs=(
            P("ctx", "exp"),
            P("ctx", "exp"),
            P("ctx", "exp"),
            P("ctx", "exp"),
            P("exp"),
            P(("ctx", "exp"), None),
            P(("ctx", "exp"), None),
            P(("ctx", "exp"), None),
            P("exp", "ctx", None),
            P("exp", "ctx", None),
            P("exp", None, "ctx"),
        ),
        out_specs=P(("ctx", "exp"), None),
        check_vma=False,
    )
```

```python
import functools

import jax
import jax.numpy as jnp
from jax import lax
from jax.experimental import pallas as pl
from jax.experimental.pallas import tpu as pltpu
from jax.sharding import PartitionSpec as P

MESH = pl.DeviceIdType.MESH
F32, BF16 = jnp.float32, jnp.bfloat16
PRECISE = lax.Precision.HIGHEST
EPSILON = 1e-06
NZ, NE = 16, 32
HD, BL, SEC, ROWS, DS, FFE = 128, 512, 1024, 32, 256, 768
TILES = SEC // 128
CHUNK = 64
HALF = NZ // 2
SUBS = 4
FAR = sorted(range(1, NZ), key=lambda i: (-min(i, NZ - i), i))
WIDE = 2 * FFE // SUBS


def dot(a, b, **kw):
    return jnp.dot(a, b, preferred_element_type=F32, **kw)


def dot_t(a, b):
    return lax.dot_general(a, b, (((1,), (1,)), ((), ())), preferred_element_type=F32)


def t_dot(a, b):
    return lax.dot_general(a, b, (((0,), (0,)), ((), ())), preferred_element_type=F32)


def iota(shape, dim):
    return lax.broadcasted_iota(jnp.int32, shape, dim)


def kernel(
    q_hbm, k_hbm, v_hbm, decay_hbm, gain_hbm, res_hbm, ids_hbm, gw_hbm, wg_hbm, wu_hbm, wd_hbm,
    out_ref,
    q_ref, k_ref, v_ref, decay_ref, gain_ref, res_ref, ids_ref, gw_ref, wg_ref, wu_ref, wd_ref,
    info, pieces, gathered, entering, incoming, within, normed, heads, hidden, zrows, place, unplace,
    slots, erows, own_r, own_l, send_r, recv_r, send_l, recv_l, act, produced, fromexp, yrows, yback,
    s_in, s_wd, r_wd, s_info, r_info, s_pc, r_pc, s_en, r_en, s_hd, r_hd, s_zr, r_zr, s_sl, r_sl,
    s_rr, r_rr, s_rl, r_rl, s_ac, r_ac, s_pr, r_pr, s_yb, r_yb,
):
    z, e = lax.axis_index("ctx"), lax.axis_index("exp")
    right, left = lax.rem(z + 1, NZ), lax.rem(z + NZ - 1, NZ)
    chip = e // 2
    half, parity = z // 8, lax.rem(z, 2)
    partner = z + 1 - 2 * parity

    def remote(src, dst, ss, rs, to_z, to_e):
        return pltpu.make_async_remote_copy(
            src_ref=src, dst_ref=dst, send_sem=ss, recv_sem=rs,
            device_id=(to_z, to_e), device_id_type=MESH,
        )

    def loop(lo, hi, body):
        def step(i, c):
            body(i)
            return c
        lax.fori_loop(lo, hi, step, 0)

    drains = []

    def finish():
        for d in drains:
            d()
        drains.clear()

    staged = {}
    for n, (src, dst) in enumerate((
        (decay_hbm, decay_ref), (ids_hbm, ids_ref), (k_hbm, k_ref), (v_hbm, v_ref), (q_hbm, q_ref),
        (gain_hbm, gain_ref), (res_hbm, res_ref), (wg_hbm, wg_ref), (wu_hbm, wu_ref),
        (wd_hbm, wd_ref.at[parity]), (gw_hbm, gw_ref),
    )):
        copy = pltpu.make_async_copy(src, dst, s_in.at[n])
        staged[id(wd_ref) if src is wd_hbm else id(dst)] = copy
        copy.start()

    def need(*refs):
        for ref in refs:
            staged.pop(id(ref)).wait()

    barrier = pltpu.get_barrier_semaphore()
    for i in FAR:
        pl.semaphore_signal(
            barrier, inc=1, device_id=(lax.rem(z + i, NZ), e), device_id_type=MESH)
    loop(1, NE, lambda i: pl.semaphore_signal(
        barrier, inc=1, device_id=(z, lax.rem(e + i, NE)), device_id_type=MESH))

    lane, sub = iota((ROWS, 128), 1), iota((ROWS, 128), 0)
    eye = iota((ROWS, ROWS), 1) == iota((ROWS, ROWS), 0)
    need(decay_ref, ids_ref)
    ids_col = jnp.sum(jnp.where(eye, ids_ref[...].astype(F32), 0.0), axis=1, keepdims=True)
    near = lax.rem(lane, ROWS)
    ids_row = jnp.sum(jnp.where(sub == near, ids_col, 0.0), axis=0, keepdims=True)
    same = jnp.where((ids_col == ids_row) & (sub < near), 1.0, 0.0)
    slot_row = ids_row * 32.0 + jnp.sum(same, axis=0, keepdims=True)

    decay = jnp.concatenate([decay_ref[:, 128 * r:128 * r + 128] for r in range(TILES)], axis=0)
    upto = jnp.where(iota((128, 128), 0) <= iota((128, 128), 1), 1.0, 0.0)
    cum = dot(decay, upto, precision=PRECISE)
    tails = [jnp.zeros((1, 1), F32)]
    for r in range(1, TILES):
        tails.append(jnp.where(r % 4 == 0, 0.0, tails[r - 1] + cum[r - 1:r, 127:128]))
    running = cum + jnp.concatenate(tails, axis=0)
    running_col = running.T
    ends = [running[4 * b + 3:4 * b + 4, 127:128] for b in range(2)]
    total = ends[0] + ends[1]

    need(k_ref, v_ref)
    updates = []
    for b in range(2):
        rest = jnp.concatenate(
            [jnp.exp(ends[b] - running_col[:, 4 * b + r:4 * b + r + 1]) for r in range(4)], axis=0
        )
        decayed = (v_ref[BL * b:BL * b + BL, :].astype(F32) * rest).astype(BF16)
        updates.append(t_dot(k_ref[BL * b:BL * b + BL, :], decayed))
    own_state = jnp.exp(ends[1]) * updates[0] + updates[1]

    info[z] = jnp.concatenate([slot_row, jnp.broadcast_to(total, (1, 128))], axis=0)
    pieces[...] = own_state.reshape(NZ, 8, HD)
    pl.semaphore_wait(barrier, NZ - 1 + NE - 1)

    def turn(i):
        return lax.rem(z + i, NZ)

    def cp_info(i):
        return remote(info.at[z], info.at[z], s_info.at[i], r_info.at[i], turn(i), e)

    def cp_piece(i):
        return remote(pieces.at[turn(i)], gathered.at[z], s_pc.at[i], r_pc.at[i], turn(i), e)

    def cp_enter(i):
        return remote(entering.at[turn(i)], incoming.at[z], s_en.at[i], r_en.at[i], turn(i), e)

    def fetched(cp):
        drains.append(lambda: loop(1, NZ, lambda i: cp(i).wait_send()))

    for i in FAR:
        cp_piece(i).start()
        cp_info(i).start()
    fetched(cp_piece)
    fetched(cp_info)
    gathered[z] = pieces[z]

    cp_down = remote(wd_ref.at[parity], wd_ref.at[parity], s_wd, r_wd, partner, e)
    need(wd_ref)
    cp_down.start()
    drains.append(lambda: cp_down.wait())

    need(q_ref)
    triangle = iota((128, 128), 0) >= iota((128, 128), 1)

    def inside(r):
        b, i = divmod(r, 4)
        rows, span = pl.ds(128 * r, 128), pl.ds(BL * b, 128 * (i + 1))
        scores = dot_t(q_ref[rows, :], k_ref[span, :])
        col = running_col[:, r:r + 1]
        weights = []
        for j in range(i + 1):
            spread = col - running[4 * b + j:4 * b + j + 1, :]
            if j == i:
                spread = jnp.where(triangle, spread, -jnp.inf)
            weights.append((scores[:, 128 * j:128 * j + 128] * jnp.exp(spread)).astype(BF16))
        weights = jnp.concatenate(weights, axis=1) if i else weights[0]
        within[rows, :] = dot(weights, v_ref[span, :])

    for r in range(4):
        inside(r)

    loop(1, NZ, lambda i: cp_info(i).wait_recv())
    factors = jnp.exp(info[:, 1, :])
    loop(1, NZ, lambda i: cp_piece(i).wait_recv())
    carried = jnp.zeros((8, HD), F32)
    for n in range(NZ):
        entering[n] = carried
        carried = factors[n:n + 1, :] * carried + gathered[n]
    for i in FAR:
        cp_enter(i).start()
    fetched(cp_enter)
    incoming[z] = entering[z]
    for r in range(4, 8):
        inside(r)
    need(gain_ref)
    gain = gain_ref[...]
    loop(1, NZ, lambda i: cp_enter(i).wait_recv())
    first = incoming[...].reshape(HD, HD)

    for b in range(2):
        state = first if b == 0 else updates[0] + jnp.exp(ends[0]) * first
        state = state.astype(BF16)
        for i in range(4):
            r = 4 * b + i
            rows = pl.ds(128 * r, 128)
            across = dot(q_ref[rows, :], state) * jnp.exp(running_col[:, r:r + 1])
            attention = within[rows, :] + across
            scale = lax.rsqrt(jnp.mean(attention * attention, axis=1, keepdims=True) + EPSILON)
            normed[rows, :] = (attention * scale * gain).astype(BF16)

    def cp_heads(to):
        return remote(normed.at[pl.ds(pl.multiple_of(to * ROWS, ROWS), ROWS)], heads.at[e],
                      s_hd.at[to], r_hd.at[e], z, to)

    def cp_heads_from(frm):
        return remote(normed.at[pl.ds(0, ROWS)], heads.at[frm], s_hd.at[frm], r_hd.at[frm], z, frm)

    heads[e] = normed[pl.ds(pl.multiple_of(e * ROWS, ROWS), ROWS), :]

    def send_heads(p):
        to_chip = lax.rem(chip - z - p + 2 * NZ, NZ)
        for core in range(2):
            to = 2 * to_chip + core

            @pl.when(to != e)
            def _():
                cp_heads(to).start()

    loop(0, NZ, send_heads)
    drains.append(lambda: loop(1, NE, lambda i: cp_heads(lax.rem(e + i, NE)).wait_send()))

    quart = iota((1, 128), 1) // 32
    picks = []
    for g in range(4):
        row = jnp.zeros((1, 128), F32)
        for n in range(4):
            row += jnp.where(quart == n, info[4 * g + n, 0:1, :] + 2.0 * (4 * g + n), 0.0)
        picks.append(row)
    picks_row = jnp.concatenate(picks, axis=1).astype(jnp.int32)
    for t in range(8):
        place[128 * t:128 * t + 128, :] = jnp.where(
            iota((128, NZ * ROWS), 0) + 128 * t == picks_row, 1.0, 0.0
        ).astype(BF16)

    def cp_rows(to):
        return remote(hidden.at[to], zrows.at[z], s_zr.at[to], r_zr.at[z], to, e)

    def cp_rows_from(frm):
        return remote(hidden.at[frm], zrows.at[frm], s_zr.at[frm], r_zr.at[frm], frm, e)

    need(res_ref)

    def send_rows(p):
        odd = lax.rem(p, 2)
        c = lax.rem(z + HALF + (1 - odd) * (p // 2) - odd * ((p + 1) // 2), NZ)
        for core in range(2):
            @pl.when(2 * c + core != e)
            def _():
                cp_heads_from(2 * c + core).wait_recv()

        both = jnp.concatenate([heads[2 * c], heads[2 * c + 1]], axis=1).astype(F32)
        block = res_ref[:, pl.ds(pl.multiple_of(c * DS, DS), DS)].astype(F32)
        hidden[c] = (block + both).astype(BF16)

        @pl.when(c != z)
        def _():
            cp_rows(c).start()

    loop(0, NZ, send_rows)
    zrows[z] = hidden[z]
    drains.append(lambda: loop(1, NZ, lambda i: cp_rows(lax.rem(z + i, NZ)).wait_send()))
    need(wg_ref, wu_ref)
    loop(1, NZ, lambda i: cp_rows_from(lax.rem(z + i, NZ)).wait_recv())
    slots[...] = dot(place[...], zrows[...].reshape(NZ * ROWS, DS)).astype(BF16)

    def cp_slots(to):
        return remote(slots.at[pl.ds(pl.multiple_of(to * 32, 32), 32)], erows.at[e],
                      s_sl.at[to], r_sl.at[e], z, to)

    def cp_slots_from(frm):
        return remote(slots.at[pl.ds(0, 32)], erows.at[frm], s_sl.at[frm], r_sl.at[frm], z, frm)

    erows[e] = slots[pl.ds(pl.multiple_of(e * 32, 32), 32), :]

    def send_slots(p):
        turn = lax.rem(p, 2)
        ahead = turn * (HALF + 1 + p // 2) + (1 - turn) * (HALF - p // 2)
        to_chip = lax.rem(chip - z - ahead + 2 * NZ, NZ)
        for core in range(2):
            to = 2 * to_chip + core

            @pl.when(to != e)
            def _():
                cp_slots(to).start()

    loop(0, NZ, send_slots)
    drains.append(lambda: loop(1, NE, lambda i: cp_slots(lax.rem(e + i, NE)).wait_send()))

    def make_unplace():
        mine = jnp.where(parity == 0, picks_row[:, 0:8 * ROWS], picks_row[:, 8 * ROWS:])
        mine = mine - 16 * parity - 16 * (mine // 32)
        for g in range(2):
            lanes = jnp.broadcast_to(mine[:, 128 * g:128 * g + 128], (128, 128))
            diagonal = iota((128, 128), 0) == iota((128, 128), 1)
            col = jnp.sum(jnp.where(diagonal, lanes, 0), axis=1, keepdims=True)
            unplace[128 * g:128 * g + 128, :] = jnp.where(
                iota((128, NE * 16), 1) == col, 1.0, 0.0
            ).astype(BF16)

    def source(j):
        return lax.rem(j + chip, NZ)

    def columns(u):
        side, off = divmod(u * WIDE, FFE)
        return (wg_ref, wu_ref)[side][:, off:off + WIDE]

    def own(j, into):
        c = source(j)
        for core in range(2):
            @pl.when(2 * c + core != e)
            def _():
                cp_slots_from(2 * c + core).wait_recv()

        rows = erows[pl.ds(2 * c, 2)].reshape(CHUNK, DS)
        for u in range(SUBS):
            into[u] = dot(rows, columns(u)).astype(BF16)

    def cp_right(s, u):
        return remote(send_r.at[s, u], recv_r.at[s, u], s_rr.at[s, u], r_rr.at[s, u], right, e)

    def cp_left(s, u):
        return remote(send_l.at[s, u], recv_l.at[s, u], s_rl.at[s, u], r_rl.at[s, u], left, e)

    own(turn(HALF), own_r)
    for u in range(SUBS):
        box, cp = (send_r, cp_right) if u < SUBS // 2 else (send_l, cp_left)
        box[0, u] = own_r[u]
        cp(0, u).start()
    for s in range(1, HALF + 1):
        own(turn(HALF - s), own_r)
        if s < HALF:
            own(turn(HALF + s), own_l)
        if s == 2:
            finish()
        if s == 3:
            make_unplace()
        if s == HALF:
            break
        for u in range(SUBS):
            for box, mine, came, cp, first_half in (
                (send_r, own_r, recv_r, cp_right, True), (send_l, own_l, recv_l, cp_left, False),
            ):
                if s == 1 and (u < SUBS // 2) != first_half:
                    box[s, u] = mine[u]
                else:
                    cp(s - 1, u).wait_recv()
                    box[s, u] = (mine[u].astype(F32) + came[s - 1, u].astype(F32)).astype(BF16)
                cp(s, u).start()
    for u in range(SUBS):
        for s in range(HALF):
            if s or u < SUBS // 2:
                drains.append(lambda s=s, u=u: cp_right(s, u).wait_send())
            if s or u >= SUBS // 2:
                drains.append(lambda s=s, u=u: cp_left(s, u).wait_send())
    sums = []
    for u in range(SUBS):
        cp_left(HALF - 1, u).wait_recv()
        cp_right(HALF - 1, u).wait_recv()
        sums.append(own_r[u].astype(F32) + recv_l[HALF - 1, u].astype(F32) + recv_r[HALF - 1, u].astype(F32))
    for u in range(SUBS // 2):
        gate, up = sums[u], sums[u + SUBS // 2]
        active = (gate / (1.0 + jnp.exp(-gate)) * up).astype(BF16)
        for h in range(2):
            for core in range(2):
                act[h, z, 16 * core:16 * core + 16, WIDE * u:WIDE * u + WIDE] = (
                    active[32 * core + 16 * h:32 * core + 16 * h + 16]
                )

    def parent(k):
        return max(0, k - 2)

    reach = {1: HALF, -1: HALF - 1}

    def cp_act(way, k):
        p, d = parent(k), (1 - way) // 2
        to_half = 1 - parity if k == 1 else parity
        at = act.at[to_half, lax.rem(z - way * p + NZ, NZ)]
        return remote(at, at, s_ac.at[d, k], r_ac.at[d, k], lax.rem(z + way * (k - p) + NZ, NZ), e)

    def cp_act_in(way, k):
        at = act.at[parity, lax.rem(z - way * k + NZ, NZ)]
        return remote(at, at, s_ac.at[(1 - way) // 2, k], r_ac.at[(1 - way) // 2, k], left, e)

    def forward(way, k):
        for child in range(reach[way], 0, -1):
            if parent(child) == k:
                cp_act(way, child).start()
                drains.append(lambda way=way, k=child: cp_act(way, k).wait_send())

    def cp_produced(d):
        return remote(produced.at[d], fromexp.at[e], s_pr.at[d], r_pr.at[e], z, d)

    def cp_from(i):
        frm = lax.rem(e + i, NE)
        return remote(produced.at[frm], fromexp.at[frm], s_pr.at[frm], r_pr.at[frm], z, frm)

    def down(j):
        rows = act[parity, j]
        rows = jnp.concatenate([dot(rows, wd_ref[n]).astype(BF16) for n in range(2)], axis=1)
        for core in range(2):
            d = 2 * source(j) + core
            produced[d] = rows[16 * core:16 * core + 16]

            @pl.when(d != e)
            def _():
                cp_produced(d).start()

            @pl.when(d == e)
            def _():
                fromexp[e] = produced[d]

    for way in (1, -1):
        forward(way, 0)
    waiting = [z]
    for n in range(1, HALF // 2 + 1):
        for j in waiting:
            down(j)
        waiting = []
        for k in (2 * n - 1, 2 * n):
            for way in (1, -1):
                if k <= reach[way]:
                    cp_act_in(way, k).wait_recv()
                    forward(way, k)
                    waiting.append(lax.rem(z - way * k + NZ, NZ))
    for j in waiting:
        down(j)
    drains.append(lambda: loop(1, NE, lambda i: cp_from(i).wait_send()))
    loop(1, NE, lambda i: cp_from(i).wait_recv())
    back = dot(unplace[...], fromexp[...].reshape(NE * 16, 2 * DS)).astype(BF16)
    yrows[...] = back.reshape(8, ROWS, 2 * DS)

    def cp_back(i):
        return remote(yrows.at[i], yback.at[z // 2], s_yb.at[i], r_yb.at[z // 2], 8 * parity + i, e)

    def cp_back_from(i):
        return remote(yrows.at[i], yback.at[i], s_yb.at[i], r_yb.at[i], 2 * i + half, e)

    def sent_back(act_on):
        def one(n):
            i = lax.rem(z // 2 + n, 8)

            @pl.when(8 * parity + i != z)
            def _():
                act_on(i)
        loop(0, 8, one)

    sent_back(lambda i: cp_back(i).start())
    need(gw_ref)
    gw_col = jnp.sum(jnp.where(eye, gw_ref[...], 0.0), axis=1, keepdims=True)
    finish()

    def mix(n):
        i = lax.rem(z // 2 + 8 - n, 8)

        @pl.when(2 * i + half != z)
        def _():
            cp_back_from(i).wait_recv()

        @pl.when(2 * i + half == z)
        def _():
            yback[i] = yrows[lax.rem(z, 8)]

        rows = jnp.concatenate([hidden[2 * i], hidden[2 * i + 1]], axis=1).astype(F32)
        mixed = rows + gw_col * yback[i].astype(F32)
        out_ref[:, pl.ds(pl.multiple_of(i * 2 * DS, 2 * DS), 2 * DS)] = mixed.astype(BF16)

    loop(0, 8, mix)
    sent_back(lambda i: cp_back(i).wait_send())


def shards(q, k, v, log_decay, gain, residual, ids, gate_weights, w_gate, w_up, w_down):
    sem = pltpu.SemaphoreType.DMA
    pair = lambda *shape: [sem(shape), sem(shape)]
    args = (
        q, k, v, log_decay.T, gain.reshape(1, HD), residual, ids.T, gate_weights.T,
        w_gate[0], w_up[0], w_down[0],
    )
    scratch = [
        *[pltpu.VMEM(a.shape, a.dtype) for a in args[:-1]],
        pltpu.VMEM((2, FFE, DS), BF16),
        pltpu.VMEM((NZ, 2, 128), F32),
        *[pltpu.VMEM((NZ, 8, HD), F32)] * 4,
        pltpu.VMEM((SEC, HD), F32),
        pltpu.VMEM((SEC, HD), BF16),
        pltpu.VMEM((NE, ROWS, HD), BF16),
        pltpu.VMEM((NZ, ROWS, DS), BF16),
        pltpu.VMEM((NZ, ROWS, DS), BF16),
        pltpu.VMEM((NE * 32, NZ * ROWS), BF16),
        pltpu.VMEM((8 * ROWS, NE * 16), BF16),
        pltpu.VMEM((NE * 32, DS), BF16),
        pltpu.VMEM((NE, 32, DS), BF16),
        pltpu.VMEM((SUBS, CHUNK, WIDE), BF16),
        pltpu.VMEM((SUBS, CHUNK, WIDE), BF16),
        pltpu.VMEM((HALF, SUBS, CHUNK, WIDE), BF16),
        pltpu.VMEM((HALF, SUBS, CHUNK, WIDE), BF16),
        pltpu.VMEM((HALF, SUBS, CHUNK, WIDE), BF16),
        pltpu.VMEM((HALF, SUBS, CHUNK, WIDE), BF16),
        pltpu.VMEM((2, NZ, CHUNK // 2, FFE), BF16),
        *[pltpu.VMEM((NE, 16, 2 * DS), BF16)] * 2,
        *[pltpu.VMEM((8, ROWS, 2 * DS), BF16)] * 2,
        sem((len(args),)),
        pltpu.SemaphoreType.DMA, pltpu.SemaphoreType.DMA,
        *pair(NZ), *pair(NZ), *pair(NZ), *pair(NE), *pair(NZ), *pair(NE),
        *pair(HALF, SUBS), *pair(HALF, SUBS), *pair(2, HALF + 1), *pair(NE), *pair(8),
    ]
    return pl.pallas_call(
        kernel,
        out_shape=jax.ShapeDtypeStruct(residual.shape, BF16),
        in_specs=[pl.BlockSpec(memory_space=pltpu.HBM)] * len(args),
        out_specs=pl.BlockSpec(memory_space=pltpu.VMEM),
        scratch_shapes=scratch,
        name="layer_pair",
        compiler_params=pltpu.CompilerParams(
            collective_id=0, has_side_effects=True, vmem_limit_bytes=60 << 20
        ),
    )(*args)


def solution(mesh):
    return jax.shard_map(
        shards,
        mesh=mesh,
        in_specs=(
            P("ctx", "exp"),
            P("ctx", "exp"),
            P("ctx", "exp"),
            P("ctx", "exp"),
            P("exp"),
            P(("ctx", "exp"), None),
            P(("ctx", "exp"), None),
            P(("ctx", "exp"), None),
            P("exp", "ctx", None),
            P("exp", "ctx", None),
            P("exp", None, "ctx"),
        ),
        out_specs=P(("ctx", "exp"), None),
        check_vma=False,
    )
```

```python
import functools

import jax
import jax.numpy as jnp
from jax import lax
from jax.experimental import pallas as pl
from jax.experimental.pallas import tpu as pltpu
from jax.sharding import PartitionSpec as P

MESH = pl.DeviceIdType.MESH
F32, BF16 = jnp.float32, jnp.bfloat16
PRECISE = lax.Precision.HIGHEST
EPSILON = 1e-06
NZ, NE = 16, 32
HD, BL, SEC, ROWS, DS, FFE = 128, 512, 1024, 32, 256, 768
TILES = SEC // 128
CHUNK = 64
HALF = NZ // 2
SUBS = 4
FAR = sorted(range(1, NZ), key=lambda i: (-min(i, NZ - i), i))
WIDE = 2 * FFE // SUBS


def dot(a, b, **kw):
    return jnp.dot(a, b, preferred_element_type=F32, **kw)


def dot_t(a, b):
    return lax.dot_general(a, b, (((1,), (1,)), ((), ())), preferred_element_type=F32)


def t_dot(a, b):
    return lax.dot_general(a, b, (((0,), (0,)), ((), ())), preferred_element_type=F32)


def iota(shape, dim):
    return lax.broadcasted_iota(jnp.int32, shape, dim)


def kernel(
    q_hbm, k_hbm, v_hbm, decay_hbm, gain_hbm, res_hbm, ids_hbm, gw_hbm, wg_hbm, wu_hbm, wd_hbm,
    out_ref,
    q_ref, k_ref, v_ref, decay_ref, gain_ref, res_ref, ids_ref, gw_ref, wg_ref, wu_ref, wd_ref,
    info, pieces, gathered, entering, incoming, within, normed, heads, hidden, zrows, place, unplace,
    slots, erows, own_r, own_l, send_r, recv_r, send_l, recv_l, act, produced, fromexp, yrows, yback,
    s_in, s_wd, r_wd, s_info, r_info, s_pc, r_pc, s_en, r_en, s_hd, r_hd, s_zr, r_zr, s_sl, r_sl,
    s_rr, r_rr, s_rl, r_rl, s_ac, r_ac, s_pr, r_pr, s_yb, r_yb,
):
    z, e = lax.axis_index("ctx"), lax.axis_index("exp")
    right, left = lax.rem(z + 1, NZ), lax.rem(z + NZ - 1, NZ)
    chip = e // 2
    half, parity = z // 8, lax.rem(z, 2)
    partner = z + 1 - 2 * parity

    def remote(src, dst, ss, rs, to_z, to_e):
        return pltpu.make_async_remote_copy(
            src_ref=src, dst_ref=dst, send_sem=ss, recv_sem=rs,
            device_id=(to_z, to_e), device_id_type=MESH,
        )

    def loop(lo, hi, body):
        def step(i, c):
            body(i)
            return c
        lax.fori_loop(lo, hi, step, 0)

    drains = []

    def finish():
        for d in drains:
            d()
        drains.clear()

    staged = {}
    for n, (src, dst) in enumerate((
        (decay_hbm, decay_ref), (ids_hbm, ids_ref), (k_hbm, k_ref), (v_hbm, v_ref), (q_hbm, q_ref),
        (gain_hbm, gain_ref), (res_hbm, res_ref), (wg_hbm, wg_ref), (wu_hbm, wu_ref),
        (wd_hbm, wd_ref.at[parity]), (gw_hbm, gw_ref),
    )):
        copy = pltpu.make_async_copy(src, dst, s_in.at[n])
        staged[id(wd_ref) if src is wd_hbm else id(dst)] = copy
        copy.start()

    def need(*refs):
        for ref in refs:
            staged.pop(id(ref)).wait()

    barrier = pltpu.get_barrier_semaphore()
    for i in FAR:
        pl.semaphore_signal(
            barrier, inc=1, device_id=(lax.rem(z + i, NZ), e), device_id_type=MESH)
    loop(1, NE, lambda i: pl.semaphore_signal(
        barrier, inc=1, device_id=(z, lax.rem(e + i, NE)), device_id_type=MESH))

    lane, sub = iota((ROWS, 128), 1), iota((ROWS, 128), 0)
    eye = iota((ROWS, ROWS), 1) == iota((ROWS, ROWS), 0)
    need(decay_ref, ids_ref)
    ids_col = jnp.sum(jnp.where(eye, ids_ref[...].astype(F32), 0.0), axis=1, keepdims=True)
    near = lax.rem(lane, ROWS)
    ids_row = jnp.sum(jnp.where(sub == near, ids_col, 0.0), axis=0, keepdims=True)
    same = jnp.where((ids_col == ids_row) & (sub < near), 1.0, 0.0)
    slot_row = ids_row * 32.0 + jnp.sum(same, axis=0, keepdims=True)

    decay = jnp.concatenate([decay_ref[:, 128 * r:128 * r + 128] for r in range(TILES)], axis=0)
    upto = jnp.where(iota((128, 128), 0) <= iota((128, 128), 1), 1.0, 0.0)
    cum = dot(decay, upto, precision=PRECISE)
    tails = [jnp.zeros((1, 1), F32)]
    for r in range(1, TILES):
        tails.append(jnp.where(r % 4 == 0, 0.0, tails[r - 1] + cum[r - 1:r, 127:128]))
    running = cum + jnp.concatenate(tails, axis=0)
    running_col = running.T
    ends = [running[4 * b + 3:4 * b + 4, 127:128] for b in range(2)]
    total = ends[0] + ends[1]

    need(k_ref, v_ref)
    updates = []
    for b in range(2):
        rest = jnp.concatenate(
            [jnp.exp(ends[b] - running_col[:, 4 * b + r:4 * b + r + 1]) for r in range(4)], axis=0
        )
        decayed = (v_ref[BL * b:BL * b + BL, :].astype(F32) * rest).astype(BF16)
        updates.append(t_dot(k_ref[BL * b:BL * b + BL, :], decayed))
    own_state = jnp.exp(ends[1]) * updates[0] + updates[1]

    info[z] = jnp.concatenate([slot_row, jnp.broadcast_to(total, (1, 128))], axis=0)
    pieces[...] = own_state.reshape(NZ, 8, HD)
    pl.semaphore_wait(barrier, NZ - 1 + NE - 1)

    def turn(i):
        return lax.rem(z + i, NZ)

    def cp_info(i):
        return remote(info.at[z], info.at[z], s_info.at[i], r_info.at[i], turn(i), e)

    def cp_piece(i):
        return remote(pieces.at[turn(i)], gathered.at[z], s_pc.at[i], r_pc.at[i], turn(i), e)

    def cp_enter(i):
        return remote(entering.at[turn(i)], incoming.at[z], s_en.at[i], r_en.at[i], turn(i), e)

    def fetched(cp):
        drains.append(lambda: loop(1, NZ, lambda i: cp(i).wait_send()))

    for i in FAR:
        cp_piece(i).start()
        cp_info(i).start()
    fetched(cp_piece)
    fetched(cp_info)
    gathered[z] = pieces[z]

    def cp_down(n):
        at = wd_ref.at[parity, pl.ds(DS * n, DS)]
        return remote(at, at, s_wd.at[n], r_wd.at[n], partner, e)

    need(wd_ref)
    cp_down(0).start()
    drains.append(lambda: loop(0, 3, lambda n: cp_down(n).wait()))

    need(q_ref)
    triangle = iota((128, 128), 0) >= iota((128, 128), 1)

    def inside(r):
        b, i = divmod(r, 4)
        rows, span = pl.ds(128 * r, 128), pl.ds(BL * b, 128 * (i + 1))
        scores = dot_t(q_ref[rows, :], k_ref[span, :])
        col = running_col[:, r:r + 1]
        weights = []
        for j in range(i + 1):
            spread = col - running[4 * b + j:4 * b + j + 1, :]
            if j == i:
                spread = jnp.where(triangle, spread, -jnp.inf)
            weights.append((scores[:, 128 * j:128 * j + 128] * jnp.exp(spread)).astype(BF16))
        weights = jnp.concatenate(weights, axis=1) if i else weights[0]
        within[rows, :] = dot(weights, v_ref[span, :])

    for r in range(4):
        inside(r)

    loop(1, NZ, lambda i: cp_info(i).wait_recv())
    factors = jnp.exp(info[:, 1, :])
    loop(1, NZ, lambda i: cp_piece(i).wait_recv())
    carried = jnp.zeros((8, HD), F32)
    for n in range(NZ):
        entering[n] = carried
        carried = factors[n:n + 1, :] * carried + gathered[n]
    for i in FAR:
        cp_enter(i).start()
    fetched(cp_enter)
    incoming[z] = entering[z]
    cp_down(1).start()
    for r in range(4, 8):
        inside(r)
    need(gain_ref)
    gain = gain_ref[...]
    loop(1, NZ, lambda i: cp_enter(i).wait_recv())
    first = incoming[...].reshape(HD, HD)

    for b in range(2):
        state = first if b == 0 else updates[0] + jnp.exp(ends[0]) * first
        state = state.astype(BF16)
        for i in range(4):
            r = 4 * b + i
            rows = pl.ds(128 * r, 128)
            across = dot(q_ref[rows, :], state) * jnp.exp(running_col[:, r:r + 1])
            attention = within[rows, :] + across
            scale = lax.rsqrt(jnp.mean(attention * attention, axis=1, keepdims=True) + EPSILON)
            normed[rows, :] = (attention * scale * gain).astype(BF16)

    def cp_heads(to):
        return remote(normed.at[pl.ds(pl.multiple_of(to * ROWS, ROWS), ROWS)], heads.at[e],
                      s_hd.at[to], r_hd.at[e], z, to)

    def cp_heads_from(frm):
        return remote(normed.at[pl.ds(0, ROWS)], heads.at[frm], s_hd.at[frm], r_hd.at[frm], z, frm)

    heads[e] = normed[pl.ds(pl.multiple_of(e * ROWS, ROWS), ROWS), :]

    def send_heads(p):
        to_chip = lax.rem(chip - z - p + 2 * NZ, NZ)
        for core in range(2):
            to = 2 * to_chip + core

            @pl.when(to != e)
            def _():
                cp_heads(to).start()

    loop(0, NZ, send_heads)
    cp_down(2).start()
    drains.append(lambda: loop(1, NE, lambda i: cp_heads(lax.rem(e + i, NE)).wait_send()))

    quart = iota((1, 128), 1) // 32
    picks = []
    for g in range(4):
        row = jnp.zeros((1, 128), F32)
        for n in range(4):
            row += jnp.where(quart == n, info[4 * g + n, 0:1, :] + 2.0 * (4 * g + n), 0.0)
        picks.append(row)
    picks_row = jnp.concatenate(picks, axis=1).astype(jnp.int32)
    for t in range(8):
        place[128 * t:128 * t + 128, :] = jnp.where(
            iota((128, NZ * ROWS), 0) + 128 * t == picks_row, 1.0, 0.0
        ).astype(BF16)

    def cp_rows(to):
        return remote(hidden.at[to], zrows.at[z], s_zr.at[to], r_zr.at[z], to, e)

    def cp_rows_from(frm):
        return remote(hidden.at[frm], zrows.at[frm], s_zr.at[frm], r_zr.at[frm], frm, e)

    need(res_ref)

    def send_rows(p):
        odd = lax.rem(p, 2)
        c = lax.rem(z + HALF + (1 - odd) * (p // 2) - odd * ((p + 1) // 2), NZ)
        for core in range(2):
            @pl.when(2 * c + core != e)
            def _():
                cp_heads_from(2 * c + core).wait_recv()

        both = jnp.concatenate([heads[2 * c], heads[2 * c + 1]], axis=1).astype(F32)
        block = res_ref[:, pl.ds(pl.multiple_of(c * DS, DS), DS)].astype(F32)
        hidden[c] = (block + both).astype(BF16)

        @pl.when(c != z)
        def _():
            cp_rows(c).start()

    loop(0, NZ, send_rows)
    zrows[z] = hidden[z]
    drains.append(lambda: loop(1, NZ, lambda i: cp_rows(lax.rem(z + i, NZ)).wait_send()))
    need(wg_ref, wu_ref)
    loop(1, NZ, lambda i: cp_rows_from(lax.rem(z + i, NZ)).wait_recv())
    slots[...] = dot(place[...], zrows[...].reshape(NZ * ROWS, DS)).astype(BF16)

    def cp_slots(to):
        return remote(slots.at[pl.ds(pl.multiple_of(to * 32, 32), 32)], erows.at[e],
                      s_sl.at[to], r_sl.at[e], z, to)

    def cp_slots_from(frm):
        return remote(slots.at[pl.ds(0, 32)], erows.at[frm], s_sl.at[frm], r_sl.at[frm], z, frm)

    erows[e] = slots[pl.ds(pl.multiple_of(e * 32, 32), 32), :]

    def send_slots(p):
        turn = lax.rem(p, 2)
        ahead = turn * (HALF + 1 + p // 2) + (1 - turn) * (HALF - p // 2)
        to_chip = lax.rem(chip - z - ahead + 2 * NZ, NZ)
        for core in range(2):
            to = 2 * to_chip + core

            @pl.when(to != e)
            def _():
                cp_slots(to).start()

    loop(0, NZ, send_slots)
    drains.append(lambda: loop(1, NE, lambda i: cp_slots(lax.rem(e + i, NE)).wait_send()))

    def make_unplace():
        mine = jnp.where(parity == 0, picks_row[:, 0:8 * ROWS], picks_row[:, 8 * ROWS:])
        mine = mine - 16 * parity - 16 * (mine // 32)
        for g in range(2):
            lanes = jnp.broadcast_to(mine[:, 128 * g:128 * g + 128], (128, 128))
            diagonal = iota((128, 128), 0) == iota((128, 128), 1)
            col = jnp.sum(jnp.where(diagonal, lanes, 0), axis=1, keepdims=True)
            unplace[128 * g:128 * g + 128, :] = jnp.where(
                iota((128, NE * 16), 1) == col, 1.0, 0.0
            ).astype(BF16)

    def source(j):
        return lax.rem(j + chip, NZ)

    def columns(u):
        side, off = divmod(u * WIDE, FFE)
        return (wg_ref, wu_ref)[side][:, off:off + WIDE]

    def own(j, into):
        c = source(j)
        for core in range(2):
            @pl.when(2 * c + core != e)
            def _():
                cp_slots_from(2 * c + core).wait_recv()

        rows = erows[pl.ds(2 * c, 2)].reshape(CHUNK, DS)
        for u in range(SUBS):
            into[u] = dot(rows, columns(u)).astype(BF16)

    def cp_right(s, u):
        return remote(send_r.at[s, u], recv_r.at[s, u], s_rr.at[s, u], r_rr.at[s, u], right, e)

    def cp_left(s, u):
        return remote(send_l.at[s, u], recv_l.at[s, u], s_rl.at[s, u], r_rl.at[s, u], left, e)

    own(turn(HALF), own_r)
    for u in range(SUBS):
        box, cp = (send_r, cp_right) if u < SUBS // 2 else (send_l, cp_left)
        box[0, u] = own_r[u]
        cp(0, u).start()
    for s in range(1, HALF + 1):
        own(turn(HALF - s), own_r)
        if s < HALF:
            own(turn(HALF + s), own_l)
        if s == 2:
            finish()
        if s == 3:
            make_unplace()
        if s == HALF:
            break
        for u in range(SUBS):
            for box, mine, came, cp, first_half in (
                (send_r, own_r, recv_r, cp_right, True), (send_l, own_l, recv_l, cp_left, False),
            ):
                if s == 1 and (u < SUBS // 2) != first_half:
                    box[s, u] = mine[u]
                else:
                    cp(s - 1, u).wait_recv()
                    box[s, u] = (mine[u].astype(F32) + came[s - 1, u].astype(F32)).astype(BF16)
                cp(s, u).start()
    for u in range(SUBS):
        for s in range(HALF):
            if s or u < SUBS // 2:
                drains.append(lambda s=s, u=u: cp_right(s, u).wait_send())
            if s or u >= SUBS // 2:
                drains.append(lambda s=s, u=u: cp_left(s, u).wait_send())
    sums = []
    for u in range(SUBS):
        cp_left(HALF - 1, u).wait_recv()
        cp_right(HALF - 1, u).wait_recv()
        sums.append(own_r[u].astype(F32) + recv_l[HALF - 1, u].astype(F32) + recv_r[HALF - 1, u].astype(F32))
    for u in range(SUBS // 2):
        gate, up = sums[u], sums[u + SUBS // 2]
        active = (gate / (1.0 + jnp.exp(-gate)) * up).astype(BF16)
        for h in range(2):
            for core in range(2):
                act[h, z, 16 * core:16 * core + 16, WIDE * u:WIDE * u + WIDE] = (
                    active[32 * core + 16 * h:32 * core + 16 * h + 16]
                )

    def parent(k):
        return max(0, k - 2)

    reach = {1: HALF, -1: HALF - 1}

    def cp_act(way, k):
        p, d = parent(k), (1 - way) // 2
        to_half = 1 - parity if k == 1 else parity
        at = act.at[to_half, lax.rem(z - way * p + NZ, NZ)]
        return remote(at, at, s_ac.at[d, k], r_ac.at[d, k], lax.rem(z + way * (k - p) + NZ, NZ), e)

    def cp_act_in(way, k):
        at = act.at[parity, lax.rem(z - way * k + NZ, NZ)]
        return remote(at, at, s_ac.at[(1 - way) // 2, k], r_ac.at[(1 - way) // 2, k], left, e)

    def forward(way, k):
        for child in range(reach[way], 0, -1):
            if parent(child) == k:
                cp_act(way, child).start()
                drains.append(lambda way=way, k=child: cp_act(way, k).wait_send())

    def cp_produced(d):
        return remote(produced.at[d], fromexp.at[e], s_pr.at[d], r_pr.at[e], z, d)

    def cp_from(i):
        frm = lax.rem(e + i, NE)
        return remote(produced.at[frm], fromexp.at[frm], s_pr.at[frm], r_pr.at[frm], z, frm)

    def down(j):
        rows = act[parity, j]
        rows = jnp.concatenate([dot(rows, wd_ref[n]).astype(BF16) for n in range(2)], axis=1)
        for core in range(2):
            d = 2 * source(j) + core
            produced[d] = rows[16 * core:16 * core + 16]

            @pl.when(d != e)
            def _():
                cp_produced(d).start()

            @pl.when(d == e)
            def _():
                fromexp[e] = produced[d]

    for way in (1, -1):
        forward(way, 0)
    waiting = [z]
    for n in range(1, HALF // 2 + 1):
        for j in waiting:
            down(j)
        waiting = []
        for k in (2 * n - 1, 2 * n):
            for way in (1, -1):
                if k <= reach[way]:
                    cp_act_in(way, k).wait_recv()
                    forward(way, k)
                    waiting.append(lax.rem(z - way * k + NZ, NZ))
    for j in waiting:
        down(j)
    drains.append(lambda: loop(1, NE, lambda i: cp_from(i).wait_send()))
    loop(1, NE, lambda i: cp_from(i).wait_recv())
    back = dot(unplace[...], fromexp[...].reshape(NE * 16, 2 * DS)).astype(BF16)
    yrows[...] = back.reshape(8, ROWS, 2 * DS)

    def cp_back(i):
        return remote(yrows.at[i], yback.at[z // 2], s_yb.at[i], r_yb.at[z // 2], 8 * parity + i, e)

    def cp_back_from(i):
        return remote(yrows.at[i], yback.at[i], s_yb.at[i], r_yb.at[i], 2 * i + half, e)

    def sent_back(act_on):
        def one(n):
            i = lax.rem(z // 2 + n, 8)

            @pl.when(8 * parity + i != z)
            def _():
                act_on(i)
        loop(0, 8, one)

    sent_back(lambda i: cp_back(i).start())
    need(gw_ref)
    gw_col = jnp.sum(jnp.where(eye, gw_ref[...], 0.0), axis=1, keepdims=True)
    finish()

    def mix(n):
        i = lax.rem(z // 2 + 8 - n, 8)

        @pl.when(2 * i + half != z)
        def _():
            cp_back_from(i).wait_recv()

        @pl.when(2 * i + half == z)
        def _():
            yback[i] = yrows[lax.rem(z, 8)]

        rows = jnp.concatenate([hidden[2 * i], hidden[2 * i + 1]], axis=1).astype(F32)
        mixed = rows + gw_col * yback[i].astype(F32)
        out_ref[:, pl.ds(pl.multiple_of(i * 2 * DS, 2 * DS), 2 * DS)] = mixed.astype(BF16)

    loop(0, 8, mix)
    sent_back(lambda i: cp_back(i).wait_send())


def shards(q, k, v, log_decay, gain, residual, ids, gate_weights, w_gate, w_up, w_down):
    sem = pltpu.SemaphoreType.DMA
    pair = lambda *shape: [sem(shape), sem(shape)]
    args = (
        q, k, v, log_decay.T, gain.reshape(1, HD), residual, ids.T, gate_weights.T,
        w_gate[0], w_up[0], w_down[0],
    )
    scratch = [
        *[pltpu.VMEM(a.shape, a.dtype) for a in args[:-1]],
        pltpu.VMEM((2, FFE, DS), BF16),
        pltpu.VMEM((NZ, 2, 128), F32),
        *[pltpu.VMEM((NZ, 8, HD), F32)] * 4,
        pltpu.VMEM((SEC, HD), F32),
        pltpu.VMEM((SEC, HD), BF16),
        pltpu.VMEM((NE, ROWS, HD), BF16),
        pltpu.VMEM((NZ, ROWS, DS), BF16),
        pltpu.VMEM((NZ, ROWS, DS), BF16),
        pltpu.VMEM((NE * 32, NZ * ROWS), BF16),
        pltpu.VMEM((8 * ROWS, NE * 16), BF16),
        pltpu.VMEM((NE * 32, DS), BF16),
        pltpu.VMEM((NE, 32, DS), BF16),
        pltpu.VMEM((SUBS, CHUNK, WIDE), BF16),
        pltpu.VMEM((SUBS, CHUNK, WIDE), BF16),
        pltpu.VMEM((HALF, SUBS, CHUNK, WIDE), BF16),
        pltpu.VMEM((HALF, SUBS, CHUNK, WIDE), BF16),
        pltpu.VMEM((HALF, SUBS, CHUNK, WIDE), BF16),
        pltpu.VMEM((HALF, SUBS, CHUNK, WIDE), BF16),
        pltpu.VMEM((2, NZ, CHUNK // 2, FFE), BF16),
        *[pltpu.VMEM((NE, 16, 2 * DS), BF16)] * 2,
        *[pltpu.VMEM((8, ROWS, 2 * DS), BF16)] * 2,
        sem((len(args),)),
        *pair(3),
        *pair(NZ), *pair(NZ), *pair(NZ), *pair(NE), *pair(NZ), *pair(NE),
        *pair(HALF, SUBS), *pair(HALF, SUBS), *pair(2, HALF + 1), *pair(NE), *pair(8),
    ]
    return pl.pallas_call(
        kernel,
        out_shape=jax.ShapeDtypeStruct(residual.shape, BF16),
        in_specs=[pl.BlockSpec(memory_space=pltpu.HBM)] * len(args),
        out_specs=pl.BlockSpec(memory_space=pltpu.VMEM),
        scratch_shapes=scratch,
        name="layer_pair",
        compiler_params=pltpu.CompilerParams(
            collective_id=0, has_side_effects=True, vmem_limit_bytes=54848 << 10
        ),
    )(*args)


def solution(mesh):
    return jax.shard_map(
        shards,
        mesh=mesh,
        in_specs=(
            P("ctx", "exp"),
            P("ctx", "exp"),
            P("ctx", "exp"),
            P("ctx", "exp"),
            P("exp"),
            P(("ctx", "exp"), None),
            P(("ctx", "exp"), None),
            P(("ctx", "exp"), None),
            P("exp", "ctx", None),
            P("exp", "ctx", None),
            P("exp", None, "ctx"),
        ),
        out_specs=P(("ctx", "exp"), None),
        check_vma=False,
    )
```

```python
import functools

import jax
import jax.numpy as jnp
from jax import lax
from jax.experimental import pallas as pl
from jax.experimental.pallas import tpu as pltpu
from jax.sharding import PartitionSpec as P

MESH = pl.DeviceIdType.MESH
F32, BF16 = jnp.float32, jnp.bfloat16
PRECISE = lax.Precision.HIGHEST
EPSILON = 1e-06
NZ, NE = 16, 32
HD, BL, SEC, ROWS, DS, FFE = 128, 512, 1024, 32, 256, 768
TILES = SEC // 128
CHUNK = 64
HALF = NZ // 2
SUBS = 4
FAR = sorted(range(1, NZ), key=lambda i: (-min(i, NZ - i), i))
WIDE = 2 * FFE // SUBS


def dot(a, b, **kw):
    return jnp.dot(a, b, preferred_element_type=F32, **kw)


def dot_t(a, b):
    return lax.dot_general(a, b, (((1,), (1,)), ((), ())), preferred_element_type=F32)


def t_dot(a, b):
    return lax.dot_general(a, b, (((0,), (0,)), ((), ())), preferred_element_type=F32)


def iota(shape, dim):
    return lax.broadcasted_iota(jnp.int32, shape, dim)


def kernel(
    q_hbm, k_hbm, v_hbm, decay_hbm, gain_hbm, res_hbm, ids_hbm, gw_hbm, wg_hbm, wu_hbm, wd_hbm,
    out_ref,
    q_ref, k_ref, v_ref, decay_ref, gain_ref, res_ref, ids_ref, gw_ref, wg_ref, wu_ref, wd_ref,
    info, pieces, gathered, entering, incoming, within, normed, heads, hidden, zrows, place, unplace,
    slots, erows, own_r, own_l, send_r, recv_r, send_l, recv_l, act, produced, fromexp, yrows, yback,
    s_in, s_wd, r_wd, s_info, r_info, s_pc, r_pc, s_en, r_en, s_hd, r_hd, s_zr, r_zr, s_sl, r_sl,
    s_rr, r_rr, s_rl, r_rl, s_ac, r_ac, s_pr, r_pr, s_yb, r_yb,
):
    z, e = lax.axis_index("ctx"), lax.axis_index("exp")
    right, left = lax.rem(z + 1, NZ), lax.rem(z + NZ - 1, NZ)
    chip = e // 2
    half, parity = z // 8, lax.rem(z, 2)
    partner = z + 1 - 2 * parity

    def remote(src, dst, ss, rs, to_z, to_e):
        return pltpu.make_async_remote_copy(
            src_ref=src, dst_ref=dst, send_sem=ss, recv_sem=rs,
            device_id=(to_z, to_e), device_id_type=MESH,
        )

    def loop(lo, hi, body):
        def step(i, c):
            body(i)
            return c
        lax.fori_loop(lo, hi, step, 0)

    drains = []

    def finish():
        for d in drains:
            d()
        drains.clear()

    staged = {}
    for n, (src, dst) in enumerate((
        (decay_hbm, decay_ref), (ids_hbm, ids_ref), (k_hbm, k_ref), (v_hbm, v_ref), (q_hbm, q_ref),
        (gain_hbm, gain_ref), (res_hbm, res_ref), (wg_hbm, wg_ref), (wu_hbm, wu_ref),
        (wd_hbm, wd_ref.at[parity]), (gw_hbm, gw_ref),
    )):
        copy = pltpu.make_async_copy(src, dst, s_in.at[n])
        staged[id(wd_ref) if src is wd_hbm else id(dst)] = copy
        copy.start()

    def need(*refs):
        for ref in refs:
            staged.pop(id(ref)).wait()

    barrier = pltpu.get_barrier_semaphore()
    for i in FAR:
        pl.semaphore_signal(
            barrier, inc=1, device_id=(lax.rem(z + i, NZ), e), device_id_type=MESH)
    loop(1, NE, lambda i: pl.semaphore_signal(
        barrier, inc=1, device_id=(z, lax.rem(e + i, NE)), device_id_type=MESH))

    lane, sub = iota((ROWS, 128), 1), iota((ROWS, 128), 0)
    eye = iota((ROWS, ROWS), 1) == iota((ROWS, ROWS), 0)
    need(decay_ref, ids_ref)
    ids_col = jnp.sum(jnp.where(eye, ids_ref[...].astype(F32), 0.0), axis=1, keepdims=True)
    near = lax.rem(lane, ROWS)
    ids_row = jnp.sum(jnp.where(sub == near, ids_col, 0.0), axis=0, keepdims=True)
    same = jnp.where((ids_col == ids_row) & (sub < near), 1.0, 0.0)
    slot_row = ids_row * 32.0 + jnp.sum(same, axis=0, keepdims=True)

    decay = jnp.concatenate([decay_ref[:, 128 * r:128 * r + 128] for r in range(TILES)], axis=0)
    upto = jnp.where(iota((128, 128), 0) <= iota((128, 128), 1), 1.0, 0.0)
    cum = dot(decay, upto, precision=PRECISE)
    tails = [jnp.zeros((1, 1), F32)]
    for r in range(1, TILES):
        tails.append(jnp.where(r % 4 == 0, 0.0, tails[r - 1] + cum[r - 1:r, 127:128]))
    running = cum + jnp.concatenate(tails, axis=0)
    running_col = running.T
    ends = [running[4 * b + 3:4 * b + 4, 127:128] for b in range(2)]
    total = ends[0] + ends[1]

    need(k_ref, v_ref)
    updates = []
    for b in range(2):
        rest = jnp.concatenate(
            [jnp.exp(ends[b] - running_col[:, 4 * b + r:4 * b + r + 1]) for r in range(4)], axis=0
        )
        decayed = (v_ref[BL * b:BL * b + BL, :].astype(F32) * rest).astype(BF16)
        updates.append(t_dot(k_ref[BL * b:BL * b + BL, :], decayed))
    own_state = jnp.exp(ends[1]) * updates[0] + updates[1]

    info[z] = jnp.concatenate([slot_row, jnp.broadcast_to(total, (1, 128))], axis=0)
    pieces[...] = own_state.reshape(8, 16, HD).astype(BF16)
    pl.semaphore_wait(barrier, NZ - 1 + NE - 1)

    def turn(i):
        return lax.rem(z + i, NZ)

    def cp_info(i):
        return remote(info.at[z], info.at[z], s_info.at[i], r_info.at[i], turn(i), e)

    def cp_piece(i):
        return remote(pieces.at[lax.rem(turn(i), 8)], gathered.at[z], s_pc.at[i], r_pc.at[i], turn(i), e)

    def cp_enter(i):
        return remote(entering.at[turn(i)], incoming.at[lax.rem(z, 8)], s_en.at[i], r_en.at[i], turn(i), e)

    def fetched(cp):
        drains.append(lambda: loop(1, NZ, lambda i: cp(i).wait_send()))

    for i in FAR:
        cp_piece(i).start()
        cp_info(i).start()
    fetched(cp_piece)
    fetched(cp_info)
    gathered[z] = pieces[lax.rem(z, 8)]

    def cp_down(n):
        at = wd_ref.at[parity, pl.ds(DS * n, DS)]
        return remote(at, at, s_wd.at[n], r_wd.at[n], partner, e)

    need(wd_ref)
    cp_down(0).start()
    drains.append(lambda: cp_down(0).wait())

    need(q_ref)
    triangle = iota((128, 128), 0) >= iota((128, 128), 1)

    def inside(r):
        b, i = divmod(r, 4)
        rows, span = pl.ds(128 * r, 128), pl.ds(BL * b, 128 * (i + 1))
        scores = dot_t(q_ref[rows, :], k_ref[span, :])
        col = running_col[:, r:r + 1]
        weights = []
        for j in range(i + 1):
            spread = col - running[4 * b + j:4 * b + j + 1, :]
            if j == i:
                spread = jnp.where(triangle, spread, -jnp.inf)
            weights.append((scores[:, 128 * j:128 * j + 128] * jnp.exp(spread)).astype(BF16))
        weights = jnp.concatenate(weights, axis=1) if i else weights[0]
        within[rows, :] = dot(weights, v_ref[span, :])

    for r in range(4):
        inside(r)

    loop(1, NZ, lambda i: cp_info(i).wait_recv())
    factors = jnp.exp(info[:, 1, :])
    loop(1, NZ, lambda i: cp_piece(i).wait_recv())
    carried = jnp.zeros((16, HD), F32)
    for n in range(NZ):
        entering[n] = carried.astype(BF16)
        carried = factors[n:n + 1, :] * carried + gathered[n].astype(F32)
    around = (12, 13, 3, 14, 2, 15, 1)
    for i in around:
        cp_enter(i).start()
        drains.append(lambda i=i: cp_enter(i).wait_send())
    incoming[lax.rem(z, 8)] = entering[z]
    cp_down(1).start()
    drains.append(lambda: cp_down(1).wait())
    for r in range(4, 8):
        inside(r)
    need(gain_ref)
    gain = gain_ref[...]
    for i in around:
        cp_enter(i).wait_recv()
    first = incoming[...].reshape(HD, HD).astype(F32)

    for b in range(2):
        state = first if b == 0 else updates[0] + jnp.exp(ends[0]) * first
        state = state.astype(BF16)
        for i in range(4):
            r = 4 * b + i
            rows = pl.ds(128 * r, 128)
            across = dot(q_ref[rows, :], state) * jnp.exp(running_col[:, r:r + 1])
            attention = within[rows, :] + across
            scale = lax.rsqrt(jnp.mean(attention * attention, axis=1, keepdims=True) + EPSILON)
            normed[rows, :] = (attention * scale * gain).astype(BF16)

    def cp_heads(to):
        return remote(normed.at[pl.ds(pl.multiple_of(to * ROWS, ROWS), ROWS)], heads.at[e],
                      s_hd.at[to], r_hd.at[e], z, to)

    def cp_heads_from(frm):
        return remote(normed.at[pl.ds(0, ROWS)], heads.at[frm], s_hd.at[frm], r_hd.at[frm], z, frm)

    heads[e] = normed[pl.ds(pl.multiple_of(e * ROWS, ROWS), ROWS), :]

    def send_heads(p):
        to_chip = lax.rem(chip - z - p + 2 * NZ, NZ)
        for core in range(2):
            to = 2 * to_chip + core

            @pl.when(to != e)
            def _():
                cp_heads(to).start()

    loop(0, NZ, send_heads)
    cp_down(2).start()
    drains.append(lambda: cp_down(2).wait())
    drains.append(lambda: loop(1, NE, lambda i: cp_heads(lax.rem(e + i, NE)).wait_send()))

    quart = iota((1, 128), 1) // 32
    picks = []
    for g in range(4):
        row = jnp.zeros((1, 128), F32)
        for n in range(4):
            row += jnp.where(quart == n, info[4 * g + n, 0:1, :] + 2.0 * (4 * g + n), 0.0)
        picks.append(row)
    picks_row = jnp.concatenate(picks, axis=1).astype(jnp.int32)
    for t in range(8):
        place[128 * t:128 * t + 128, :] = jnp.where(
            iota((128, NZ * ROWS), 0) + 128 * t == picks_row, 1.0, 0.0
        ).astype(BF16)

    def cp_rows(to):
        return remote(hidden.at[to], zrows.at[z], s_zr.at[to], r_zr.at[z], to, e)

    def cp_rows_from(frm):
        return remote(hidden.at[frm], zrows.at[frm], s_zr.at[frm], r_zr.at[frm], frm, e)

    need(res_ref)

    def send_rows(p):
        odd = lax.rem(p, 2)
        c = lax.rem(z + HALF + (1 - odd) * (p // 2) - odd * ((p + 1) // 2), NZ)
        for core in range(2):
            @pl.when(2 * c + core != e)
            def _():
                cp_heads_from(2 * c + core).wait_recv()

        both = jnp.concatenate([heads[2 * c], heads[2 * c + 1]], axis=1).astype(F32)
        block = res_ref[:, pl.ds(pl.multiple_of(c * DS, DS), DS)].astype(F32)
        hidden[c] = (block + both).astype(BF16)

        @pl.when(c != z)
        def _():
            cp_rows(c).start()

    loop(0, NZ, send_rows)
    zrows[z] = hidden[z]
    drains.append(lambda: loop(1, NZ, lambda i: cp_rows(lax.rem(z + i, NZ)).wait_send()))
    need(wg_ref, wu_ref)
    loop(1, NZ, lambda i: cp_rows_from(lax.rem(z + i, NZ)).wait_recv())
    slots[...] = dot(place[...], zrows[...].reshape(NZ * ROWS, DS)).astype(BF16)

    def cp_slots(to):
        return remote(slots.at[pl.ds(pl.multiple_of(to * 32, 32), 32)], erows.at[e],
                      s_sl.at[to], r_sl.at[e], z, to)

    def cp_slots_from(frm):
        return remote(slots.at[pl.ds(0, 32)], erows.at[frm], s_sl.at[frm], r_sl.at[frm], z, frm)

    erows[e] = slots[pl.ds(pl.multiple_of(e * 32, 32), 32), :]

    def send_slots(p):
        turn = lax.rem(p, 2)
        ahead = turn * (HALF + 1 + p // 2) + (1 - turn) * (HALF - p // 2)
        to_chip = lax.rem(chip - z - ahead + 2 * NZ, NZ)
        for core in range(2):
            to = 2 * to_chip + core

            @pl.when(to != e)
            def _():
                cp_slots(to).start()

    loop(0, NZ, send_slots)
    drains.append(lambda: loop(1, NE, lambda i: cp_slots(lax.rem(e + i, NE)).wait_send()))

    def make_unplace():
        mine = jnp.where(parity == 0, picks_row[:, 0:8 * ROWS], picks_row[:, 8 * ROWS:])
        mine = mine - 16 * parity - 16 * (mine // 32)
        for g in range(2):
            lanes = jnp.broadcast_to(mine[:, 128 * g:128 * g + 128], (128, 128))
            diagonal = iota((128, 128), 0) == iota((128, 128), 1)
            col = jnp.sum(jnp.where(diagonal, lanes, 0), axis=1, keepdims=True)
            unplace[128 * g:128 * g + 128, :] = jnp.where(
                iota((128, NE * 16), 1) == col, 1.0, 0.0
            ).astype(BF16)

    def source(j):
        return lax.rem(j + chip, NZ)

    def columns(u):
        off = u // 2 * WIDE
        return (wg_ref, wu_ref)[u % 2][:, off:off + WIDE]

    def own(j, into):
        c = source(j)
        for core in range(2):
            @pl.when(2 * c + core != e)
            def _():
                cp_slots_from(2 * c + core).wait_recv()

        rows = erows[pl.ds(2 * c, 2)].reshape(CHUNK, DS)
        for u in range(SUBS):
            into[u] = dot(rows, columns(u)).astype(BF16)

    def cp_right(s, u):
        return remote(send_r.at[s, u], recv_r.at[s, u], s_rr.at[s, u], r_rr.at[s, u], right, e)

    def cp_left(s, u):
        return remote(send_l.at[s, u], recv_l.at[s, u], s_rl.at[s, u], r_rl.at[s, u], left, e)

    own(turn(HALF), own_r)
    for u in range(SUBS):
        box, cp = (send_r, cp_right) if u < SUBS // 2 else (send_l, cp_left)
        box[0, u] = own_r[u]
        cp(0, u).start()
    for s in range(1, HALF + 1):
        own(turn(HALF - s), own_r)
        if s < HALF:
            own(turn(HALF + s), own_l)
        if s == 2:
            finish()
        if s == 3:
            make_unplace()
        if s == HALF:
            break
        for u in range(SUBS):
            for box, mine, came, cp, first_half in (
                (send_r, own_r, recv_r, cp_right, True), (send_l, own_l, recv_l, cp_left, False),
            ):
                if s == 1 and (u < SUBS // 2) != first_half:
                    box[s, u] = mine[u]
                else:
                    cp(s - 1, u).wait_recv()
                    box[s, u] = (mine[u].astype(F32) + came[s - 1, u].astype(F32)).astype(BF16)
                cp(s, u).start()
    for u in range(SUBS):
        for s in range(HALF):
            if s or u < SUBS // 2:
                drains.append(lambda s=s, u=u: cp_right(s, u).wait_send())
            if s or u >= SUBS // 2:
                drains.append(lambda s=s, u=u: cp_left(s, u).wait_send())
    def parent(k):
        return max(0, k - 2)

    def reach(v, way):
        return HALF if way > 0 else HALF - 1

    def cp_act(v, way, k):
        p, d = parent(k), (1 - way) // 2
        to_half = 1 - parity if k == 1 else parity
        at = act.at[v, to_half, lax.rem(z - way * p + NZ, NZ)]
        return remote(at, at, s_ac.at[v, d, k], r_ac.at[v, d, k], lax.rem(z + way * (k - p) + NZ, NZ), e)

    def cp_act_in(v, way, k):
        d = (1 - way) // 2
        at = act.at[v, parity, lax.rem(z - way * k + NZ, NZ)]
        return remote(at, at, s_ac.at[v, d, k], r_ac.at[v, d, k], left, e)

    def forward(v, way, k):
        for child in range(reach(v, way), 0, -1):
            if parent(child) == k:
                cp_act(v, way, child).start()
                drains.append(lambda k=child: cp_act(v, way, k).wait_send())

    for v in range(SUBS // 2):
        sums = []
        for u in (2 * v, 2 * v + 1):
            cp_left(HALF - 1, u).wait_recv()
            cp_right(HALF - 1, u).wait_recv()
            sums.append(own_r[u].astype(F32) + recv_l[HALF - 1, u].astype(F32) + recv_r[HALF - 1, u].astype(F32))
        gate, up = sums
        active = (gate / (1.0 + jnp.exp(-gate)) * up).astype(BF16)
        for h in range(2):
            for core in range(2):
                act[v, h, z, 16 * core:16 * core + 16] = active[32 * core + 16 * h:32 * core + 16 * h + 16]
        for way in (1, -1):
            forward(v, way, 0)

    def cp_produced(d):
        return remote(produced.at[d], fromexp.at[e], s_pr.at[d], r_pr.at[e], z, d)

    def cp_from(i):
        frm = lax.rem(e + i, NE)
        return remote(produced.at[frm], fromexp.at[frm], s_pr.at[frm], r_pr.at[frm], z, frm)

    def down(j):
        rows = jnp.concatenate([act[v, parity, j] for v in range(SUBS // 2)], axis=1)
        rows = jnp.concatenate([dot(rows, wd_ref[n]).astype(BF16) for n in range(2)], axis=1)
        for core in range(2):
            d = 2 * source(j) + core
            produced[d] = rows[16 * core:16 * core + 16]

            @pl.when(d != e)
            def _():
                cp_produced(d).start()

            @pl.when(d == e)
            def _():
                fromexp[e] = produced[d]

    waiting = [z]
    for n in range(1, HALF // 2 + 1):
        for j in waiting:
            down(j)
        waiting = []
        for v in range(SUBS // 2):
            for k in (2 * n - 1, 2 * n):
                for way in (1, -1):
                    if k <= reach(v, way):
                        cp_act_in(v, way, k).wait_recv()
                        forward(v, way, k)
                        if v:
                            waiting.append(lax.rem(z - way * k + NZ, NZ))
    for j in waiting:
        down(j)
    drains.append(lambda: loop(1, NE, lambda i: cp_from(i).wait_send()))
    loop(1, NE, lambda i: cp_from(i).wait_recv())
    back = dot(unplace[...], fromexp[...].reshape(NE * 16, 2 * DS)).astype(BF16)
    yrows[...] = back.reshape(8, ROWS, 2 * DS)

    def cp_back(i):
        return remote(yrows.at[i], yback.at[z // 2], s_yb.at[i], r_yb.at[z // 2], 8 * parity + i, e)

    def cp_back_from(i):
        return remote(yrows.at[i], yback.at[i], s_yb.at[i], r_yb.at[i], 2 * i + half, e)

    def sent_back(act_on):
        def one(n):
            odd = lax.rem(n, 2)
            step = odd * ((n + 1) // 2) + (1 - odd) * (8 - n // 2)
            near = jnp.where(half == parity, 12 - step, step)
            i = lax.rem(z + near, 8)

            @pl.when(8 * parity + i != z)
            def _():
                act_on(i)
        loop(0, 8, one)

    sent_back(lambda i: cp_back(i).start())
    need(gw_ref)
    gw_col = jnp.sum(jnp.where(eye, gw_ref[...], 0.0), axis=1, keepdims=True)
    finish()

    def mix(n):
        i = lax.rem(z // 2 + 8 - n, 8)

        @pl.when(2 * i + half != z)
        def _():
            cp_back_from(i).wait_recv()

        @pl.when(2 * i + half == z)
        def _():
            yback[i] = yrows[lax.rem(z, 8)]

        rows = jnp.concatenate([hidden[2 * i], hidden[2 * i + 1]], axis=1).astype(F32)
        mixed = rows + gw_col * yback[i].astype(F32)
        out_ref[:, pl.ds(pl.multiple_of(i * 2 * DS, 2 * DS), 2 * DS)] = mixed.astype(BF16)

    loop(0, 8, mix)
    sent_back(lambda i: cp_back(i).wait_send())


def shards(q, k, v, log_decay, gain, residual, ids, gate_weights, w_gate, w_up, w_down):
    sem = pltpu.SemaphoreType.DMA
    pair = lambda *shape: [sem(shape), sem(shape)]
    args = (
        q, k, v, log_decay.T, gain.reshape(1, HD), residual, ids.T, gate_weights.T,
        w_gate[0], w_up[0], w_down[0],
    )
    scratch = [
        *[pltpu.VMEM(a.shape, a.dtype) for a in args[:-1]],
        pltpu.VMEM((2, FFE, DS), BF16),
        pltpu.VMEM((NZ, 2, 128), F32),
        pltpu.VMEM((8, 16, HD), BF16),
        pltpu.VMEM((NZ, 16, HD), BF16),
        pltpu.VMEM((NZ, 16, HD), BF16),
        pltpu.VMEM((8, 16, HD), BF16),
        pltpu.VMEM((SEC, HD), F32),
        pltpu.VMEM((SEC, HD), BF16),
        pltpu.VMEM((NE, ROWS, HD), BF16),
        pltpu.VMEM((NZ, ROWS, DS), BF16),
        pltpu.VMEM((NZ, ROWS, DS), BF16),
        pltpu.VMEM((NE * 32, NZ * ROWS), BF16),
        pltpu.VMEM((8 * ROWS, NE * 16), BF16),
        pltpu.VMEM((NE * 32, DS), BF16),
        pltpu.VMEM((NE, 32, DS), BF16),
        pltpu.VMEM((SUBS, CHUNK, WIDE), BF16),
        pltpu.VMEM((SUBS, CHUNK, WIDE), BF16),
        pltpu.VMEM((HALF, SUBS, CHUNK, WIDE), BF16),
        pltpu.VMEM((HALF, SUBS, CHUNK, WIDE), BF16),
        pltpu.VMEM((HALF, SUBS, CHUNK, WIDE), BF16),
        pltpu.VMEM((HALF, SUBS, CHUNK, WIDE), BF16),
        pltpu.VMEM((SUBS // 2, 2, NZ, CHUNK // 2, WIDE), BF16),
        *[pltpu.VMEM((NE, 16, 2 * DS), BF16)] * 2,
        *[pltpu.VMEM((8, ROWS, 2 * DS), BF16)] * 2,
        sem((len(args),)),
        *pair(3),
        *pair(NZ), *pair(NZ), *pair(NZ), *pair(NE), *pair(NZ), *pair(NE),
        *pair(HALF, SUBS), *pair(HALF, SUBS), *pair(SUBS // 2, 2, HALF + 1), *pair(NE), *pair(8),
    ]
    return pl.pallas_call(
        kernel,
        out_shape=jax.ShapeDtypeStruct(residual.shape, BF16),
        in_specs=[pl.BlockSpec(memory_space=pltpu.HBM)] * len(args),
        out_specs=pl.BlockSpec(memory_space=pltpu.VMEM),
        scratch_shapes=scratch,
        name="layer_pair",
        compiler_params=pltpu.CompilerParams(
            collective_id=0, has_side_effects=True, vmem_limit_bytes=54848 << 10
        ),
    )(*args)


def solution(mesh):
    return jax.shard_map(
        shards,
        mesh=mesh,
        in_specs=(
            P("ctx", "exp"),
            P("ctx", "exp"),
            P("ctx", "exp"),
            P("ctx", "exp"),
            P("exp"),
            P(("ctx", "exp"), None),
            P(("ctx", "exp"), None),
            P(("ctx", "exp"), None),
            P("exp", "ctx", None),
            P("exp", "ctx", None),
            P("exp", None, "ctx"),
        ),
        out_specs=P(("ctx", "exp"), None),
        check_vma=False,
    )
```

```python
import functools

import jax
import jax.numpy as jnp
from jax import lax
from jax.experimental import pallas as pl
from jax.experimental.pallas import tpu as pltpu
from jax.sharding import PartitionSpec as P

MESH = pl.DeviceIdType.MESH
F32, BF16 = jnp.float32, jnp.bfloat16
PRECISE = lax.Precision.HIGHEST
EPSILON = 1e-06
NZ, NE = 16, 32
HD, BL, SEC, ROWS, DS, FFE = 128, 512, 1024, 32, 256, 768
TILES = SEC // 128
CHUNK = 64
HALF = NZ // 2
SUBS = 4
FAR = sorted(range(1, NZ), key=lambda i: (-min(i, NZ - i), i))
WIDE = 2 * FFE // SUBS


def dot(a, b, **kw):
    return jnp.dot(a, b, preferred_element_type=F32, **kw)


def dot_t(a, b):
    return lax.dot_general(a, b, (((1,), (1,)), ((), ())), preferred_element_type=F32)


def t_dot(a, b):
    return lax.dot_general(a, b, (((0,), (0,)), ((), ())), preferred_element_type=F32)


def iota(shape, dim):
    return lax.broadcasted_iota(jnp.int32, shape, dim)


def kernel(
    q_hbm, k_hbm, v_hbm, decay_hbm, gain_hbm, res_hbm, ids_hbm, gw_hbm, wg_hbm, wu_hbm, wd_hbm,
    out_ref,
    q_ref, k_ref, v_ref, decay_ref, gain_ref, res_ref, ids_ref, gw_ref, wg_ref, wu_ref, wd_ref,
    info, pieces, gathered, entering, incoming, within, normed, heads, hidden, zrows, place, unplace,
    slots, erows, own_r, own_l, send_r, recv_r, send_l, recv_l, act, produced, fromexp, yrows, yback,
    s_in, s_wd, r_wd, s_info, r_info, s_pc, r_pc, s_en, r_en, s_hd, r_hd, s_zr, r_zr, s_sl, r_sl,
    s_rr, r_rr, s_rl, r_rl, s_ac, r_ac, s_pr, r_pr, s_yb, r_yb,
):
    z, e = lax.axis_index("ctx"), lax.axis_index("exp")
    right, left = lax.rem(z + 1, NZ), lax.rem(z + NZ - 1, NZ)
    chip = e // 2
    half, parity = z // 8, lax.rem(z, 2)
    partner = z + 1 - 2 * parity

    def remote(src, dst, ss, rs, to_z, to_e):
        return pltpu.make_async_remote_copy(
            src_ref=src, dst_ref=dst, send_sem=ss, recv_sem=rs,
            device_id=(to_z, to_e), device_id_type=MESH,
        )

    def loop(lo, hi, body):
        def step(i, c):
            body(i)
            return c
        lax.fori_loop(lo, hi, step, 0)

    drains = []

    def finish():
        for d in drains:
            d()
        drains.clear()

    staged = {}
    for n, (src, dst) in enumerate((
        (decay_hbm, decay_ref), (ids_hbm, ids_ref), (k_hbm, k_ref), (v_hbm, v_ref), (q_hbm, q_ref),
        (gain_hbm, gain_ref), (res_hbm, res_ref), (wg_hbm, wg_ref), (wu_hbm, wu_ref),
        (wd_hbm, wd_ref.at[parity]), (gw_hbm, gw_ref),
    )):
        copy = pltpu.make_async_copy(src, dst, s_in.at[n])
        staged[id(wd_ref) if src is wd_hbm else id(dst)] = copy
        copy.start()

    def need(*refs):
        for ref in refs:
            staged.pop(id(ref)).wait()

    barrier = pltpu.get_barrier_semaphore()
    for i in FAR:
        pl.semaphore_signal(
            barrier, inc=1, device_id=(lax.rem(z + i, NZ), e), device_id_type=MESH)
    loop(1, NE, lambda i: pl.semaphore_signal(
        barrier, inc=1, device_id=(z, lax.rem(e + i, NE)), device_id_type=MESH))

    lane, sub = iota((ROWS, 128), 1), iota((ROWS, 128), 0)
    eye = iota((ROWS, ROWS), 1) == iota((ROWS, ROWS), 0)
    need(decay_ref, ids_ref)
    ids_col = jnp.sum(jnp.where(eye, ids_ref[...].astype(F32), 0.0), axis=1, keepdims=True)
    near = lax.rem(lane, ROWS)
    ids_row = jnp.sum(jnp.where(sub == near, ids_col, 0.0), axis=0, keepdims=True)
    same = jnp.where((ids_col == ids_row) & (sub < near), 1.0, 0.0)
    slot_row = ids_row * 32.0 + jnp.sum(same, axis=0, keepdims=True)

    decay = jnp.concatenate([decay_ref[:, 128 * r:128 * r + 128] for r in range(TILES)], axis=0)
    upto = jnp.where(iota((128, 128), 0) <= iota((128, 128), 1), 1.0, 0.0)
    cum = dot(decay, upto, precision=PRECISE)
    tails = [jnp.zeros((1, 1), F32)]
    for r in range(1, TILES):
        tails.append(jnp.where(r % 4 == 0, 0.0, tails[r - 1] + cum[r - 1:r, 127:128]))
    running = cum + jnp.concatenate(tails, axis=0)
    running_col = running.T
    ends = [running[4 * b + 3:4 * b + 4, 127:128] for b in range(2)]
    total = ends[0] + ends[1]

    need(k_ref, v_ref)
    updates = []
    for b in range(2):
        rest = jnp.concatenate(
            [jnp.exp(ends[b] - running_col[:, 4 * b + r:4 * b + r + 1]) for r in range(4)], axis=0
        )
        decayed = (v_ref[BL * b:BL * b + BL, :].astype(F32) * rest).astype(BF16)
        updates.append(t_dot(k_ref[BL * b:BL * b + BL, :], decayed))
    own_state = jnp.exp(ends[1]) * updates[0] + updates[1]

    info[z] = jnp.concatenate([slot_row, jnp.broadcast_to(total, (1, 128))], axis=0)
    pieces[...] = own_state.reshape(8, 16, HD).astype(BF16)
    pl.semaphore_wait(barrier, NZ - 1 + NE - 1)

    def turn(i):
        return lax.rem(z + i, NZ)

    def cp_info(i):
        return remote(info.at[z], info.at[z], s_info.at[i], r_info.at[i], turn(i), e)

    def cp_piece(i):
        return remote(pieces.at[lax.rem(turn(i), 8)], gathered.at[z], s_pc.at[i], r_pc.at[i], turn(i), e)

    def cp_enter(i):
        return remote(entering.at[turn(i)], incoming.at[lax.rem(z, 8)], s_en.at[i], r_en.at[i], turn(i), e)

    def fetched(cp):
        drains.append(lambda: loop(1, NZ, lambda i: cp(i).wait_send()))

    for i in FAR:
        cp_piece(i).start()
        cp_info(i).start()
    fetched(cp_piece)
    fetched(cp_info)
    gathered[z] = pieces[lax.rem(z, 8)]

    def cp_down(n):
        at = wd_ref.at[parity, pl.ds(DS * n, DS)]
        return remote(at, at, s_wd.at[n], r_wd.at[n], partner, e)

    need(wd_ref)
    cp_down(0).start()
    drains.append(lambda: cp_down(0).wait())

    need(q_ref)
    triangle = iota((128, 128), 0) >= iota((128, 128), 1)

    def inside(r):
        b, i = divmod(r, 4)
        rows, span = pl.ds(128 * r, 128), pl.ds(BL * b, 128 * (i + 1))
        scores = dot_t(q_ref[rows, :], k_ref[span, :])
        col = running_col[:, r:r + 1]
        weights = []
        for j in range(i + 1):
            spread = col - running[4 * b + j:4 * b + j + 1, :]
            if j == i:
                spread = jnp.where(triangle, spread, -jnp.inf)
            weights.append((scores[:, 128 * j:128 * j + 128] * jnp.exp(spread)).astype(BF16))
        weights = jnp.concatenate(weights, axis=1) if i else weights[0]
        within[rows, :] = dot(weights, v_ref[span, :])

    for r in range(4):
        inside(r)

    loop(1, NZ, lambda i: cp_info(i).wait_recv())
    factors = jnp.exp(info[:, 1, :])
    loop(1, NZ, lambda i: cp_piece(i).wait_recv())
    carried = jnp.zeros((16, HD), F32)
    for n in range(NZ):
        entering[n] = carried.astype(BF16)
        carried = factors[n:n + 1, :] * carried + gathered[n].astype(F32)
    around = (12, 13, 3, 14, 2, 15, 1)
    for i in around:
        cp_enter(i).start()
        drains.append(lambda i=i: cp_enter(i).wait_send())
    incoming[lax.rem(z, 8)] = entering[z]
    cp_down(1).start()
    drains.append(lambda: cp_down(1).wait())
    for r in range(4, 8):
        inside(r)
    need(gain_ref)
    gain = gain_ref[...]
    for i in around:
        cp_enter(i).wait_recv()
    first = incoming[...].reshape(HD, HD).astype(F32)

    for b in range(2):
        state = first if b == 0 else updates[0] + jnp.exp(ends[0]) * first
        state = state.astype(BF16)
        for i in range(4):
            r = 4 * b + i
            rows = pl.ds(128 * r, 128)
            across = dot(q_ref[rows, :], state) * jnp.exp(running_col[:, r:r + 1])
            attention = within[rows, :] + across
            scale = lax.rsqrt(jnp.mean(attention * attention, axis=1, keepdims=True) + EPSILON)
            normed[rows, :] = (attention * scale * gain).astype(BF16)

    def cp_heads(to):
        return remote(normed.at[pl.ds(pl.multiple_of(to * ROWS, ROWS), ROWS)], heads.at[e],
                      s_hd.at[to], r_hd.at[e], z, to)

    def cp_heads_from(frm):
        return remote(normed.at[pl.ds(0, ROWS)], heads.at[frm], s_hd.at[frm], r_hd.at[frm], z, frm)

    heads[e] = normed[pl.ds(pl.multiple_of(e * ROWS, ROWS), ROWS), :]

    def send_heads(p):
        to_chip = lax.rem(chip - z - p + 2 * NZ, NZ)
        for core in range(2):
            to = 2 * to_chip + core

            @pl.when(to != e)
            def _():
                cp_heads(to).start()

    loop(0, NZ, send_heads)
    cp_down(2).start()
    drains.append(lambda: cp_down(2).wait())
    drains.append(lambda: loop(1, NE, lambda i: cp_heads(lax.rem(e + i, NE)).wait_send()))

    quart = iota((1, 128), 1) // 32
    picks = []
    for g in range(4):
        row = jnp.zeros((1, 128), F32)
        for n in range(4):
            row += jnp.where(quart == n, info[4 * g + n, 0:1, :] + 2.0 * (4 * g + n), 0.0)
        picks.append(row)
    picks_row = jnp.concatenate(picks, axis=1).astype(jnp.int32)
    for t in range(8):
        place[128 * t:128 * t + 128, :] = jnp.where(
            iota((128, NZ * ROWS), 0) + 128 * t == picks_row, 1.0, 0.0
        ).astype(BF16)

    def cp_rows(to):
        return remote(hidden.at[to], zrows.at[z], s_zr.at[to], r_zr.at[z], to, e)

    def cp_rows_from(frm):
        return remote(hidden.at[frm], zrows.at[frm], s_zr.at[frm], r_zr.at[frm], frm, e)

    need(res_ref)

    def send_rows(p):
        odd = lax.rem(p, 2)
        c = lax.rem(z + HALF + (1 - odd) * (p // 2) - odd * ((p + 1) // 2), NZ)
        for core in range(2):
            @pl.when(2 * c + core != e)
            def _():
                cp_heads_from(2 * c + core).wait_recv()

        both = jnp.concatenate([heads[2 * c], heads[2 * c + 1]], axis=1).astype(F32)
        block = res_ref[:, pl.ds(pl.multiple_of(c * DS, DS), DS)].astype(F32)
        hidden[c] = (block + both).astype(BF16)

        @pl.when(c != z)
        def _():
            cp_rows(c).start()

    loop(0, NZ, send_rows)
    zrows[z] = hidden[z]
    drains.append(lambda: loop(1, NZ, lambda i: cp_rows(lax.rem(z + i, NZ)).wait_send()))
    need(wg_ref, wu_ref)
    loop(1, NZ, lambda i: cp_rows_from(lax.rem(z + i, NZ)).wait_recv())
    slots[...] = dot(place[...], zrows[...].reshape(NZ * ROWS, DS)).astype(BF16)

    def cp_slots(to):
        return remote(slots.at[pl.ds(pl.multiple_of(to * 32, 32), 32)], erows.at[e],
                      s_sl.at[to], r_sl.at[e], z, to)

    def cp_slots_from(frm):
        return remote(slots.at[pl.ds(0, 32)], erows.at[frm], s_sl.at[frm], r_sl.at[frm], z, frm)

    erows[e] = slots[pl.ds(pl.multiple_of(e * 32, 32), 32), :]

    def send_slots(p):
        turn = lax.rem(p, 2)
        ahead = turn * (HALF + 1 + p // 2) + (1 - turn) * (HALF - p // 2)
        to_chip = lax.rem(chip - z - ahead + 2 * NZ, NZ)
        for core in range(2):
            to = 2 * to_chip + core

            @pl.when(to != e)
            def _():
                cp_slots(to).start()

    loop(0, NZ, send_slots)
    drains.append(lambda: loop(1, NE, lambda i: cp_slots(lax.rem(e + i, NE)).wait_send()))

    def make_unplace():
        mine = jnp.where(parity == 0, picks_row[:, 0:8 * ROWS], picks_row[:, 8 * ROWS:])
        mine = mine - 16 * parity - 16 * (mine // 32)
        for g in range(2):
            lanes = jnp.broadcast_to(mine[:, 128 * g:128 * g + 128], (128, 128))
            diagonal = iota((128, 128), 0) == iota((128, 128), 1)
            col = jnp.sum(jnp.where(diagonal, lanes, 0), axis=1, keepdims=True)
            unplace[128 * g:128 * g + 128, :] = jnp.where(
                iota((128, NE * 16), 1) == col, 1.0, 0.0
            ).astype(BF16)

    def source(j):
        return lax.rem(j + chip, NZ)

    def columns(u):
        off = u // 2 * WIDE
        return (wg_ref, wu_ref)[u % 2][:, off:off + WIDE]

    def own(j, into):
        c = source(j)
        for core in range(2):
            @pl.when(2 * c + core != e)
            def _():
                cp_slots_from(2 * c + core).wait_recv()

        rows = erows[pl.ds(2 * c, 2)].reshape(CHUNK, DS)
        for u in range(SUBS):
            into[u] = dot(rows, columns(u)).astype(BF16)

    def cp_right(s, u):
        return remote(send_r.at[s, u], recv_r.at[s, u], s_rr.at[s, u], r_rr.at[s, u], right, e)

    def cp_left(s, u):
        return remote(send_l.at[s, u], recv_l.at[s, u], s_rl.at[s, u], r_rl.at[s, u], left, e)

    own(turn(HALF), own_r)
    for u in range(SUBS):
        box, cp = (send_r, cp_right) if u < SUBS // 2 else (send_l, cp_left)
        box[0, u] = own_r[u]
        cp(0, u).start()
    for s in range(1, HALF + 1):
        own(turn(HALF - s), own_r)
        if s < HALF:
            own(turn(HALF + s), own_l)
        if s == 2:
            finish()
        if s == 3:
            make_unplace()
        if s == HALF:
            break
        for u in range(SUBS):
            for box, mine, came, cp, first_half in (
                (send_r, own_r, recv_r, cp_right, True), (send_l, own_l, recv_l, cp_left, False),
            ):
                if s == 1 and (u < SUBS // 2) != first_half:
                    box[s, u] = mine[u]
                else:
                    cp(s - 1, u).wait_recv()
                    box[s, u] = (mine[u].astype(F32) + came[s - 1, u].astype(F32)).astype(BF16)
                cp(s, u).start()
    for u in range(SUBS):
        for s in range(HALF):
            if s or u < SUBS // 2:
                drains.append(lambda s=s, u=u: cp_right(s, u).wait_send())
            if s or u >= SUBS // 2:
                drains.append(lambda s=s, u=u: cp_left(s, u).wait_send())
    def parent(k):
        return max(0, k - 2)

    def reach(v, way):
        return HALF if way > 0 else HALF - 1

    def cp_act(v, way, k):
        p, d = parent(k), (1 - way) // 2
        to_half = 1 - parity if k == 1 else parity
        at = act.at[v, to_half, lax.rem(z - way * p + NZ, NZ)]
        return remote(at, at, s_ac.at[v, d, k], r_ac.at[v, d, k], lax.rem(z + way * (k - p) + NZ, NZ), e)

    def cp_act_in(v, way, k):
        d = (1 - way) // 2
        at = act.at[v, parity, lax.rem(z - way * k + NZ, NZ)]
        return remote(at, at, s_ac.at[v, d, k], r_ac.at[v, d, k], left, e)

    def forward(v, way, k):
        for child in range(reach(v, way), 0, -1):
            if parent(child) == k:
                cp_act(v, way, child).start()
                drains.append(lambda k=child: cp_act(v, way, k).wait_send())

    for v in range(SUBS // 2):
        sums = []
        for u in (2 * v, 2 * v + 1):
            cp_left(HALF - 1, u).wait_recv()
            cp_right(HALF - 1, u).wait_recv()
            sums.append(own_r[u].astype(F32) + recv_l[HALF - 1, u].astype(F32) + recv_r[HALF - 1, u].astype(F32))
        gate, up = sums
        active = (gate / (1.0 + jnp.exp(-gate)) * up).astype(BF16)
        for h in range(2):
            for core in range(2):
                act[v, h, z, 16 * core:16 * core + 16] = active[32 * core + 16 * h:32 * core + 16 * h + 16]
        for way in (1, -1):
            forward(v, way, 0)

    def cp_produced(d):
        return remote(produced.at[d], fromexp.at[e], s_pr.at[d], r_pr.at[e], z, d)

    def cp_from(i):
        frm = lax.rem(e + i, NE)
        return remote(produced.at[frm], fromexp.at[frm], s_pr.at[frm], r_pr.at[frm], z, frm)

    def down(j):
        rows = jnp.concatenate([act[v, parity, j] for v in range(SUBS // 2)], axis=1)
        rows = jnp.concatenate([dot(rows, wd_ref[n]).astype(BF16) for n in range(2)], axis=1)
        for core in range(2):
            d = 2 * source(j) + core
            produced[d] = rows[16 * core:16 * core + 16]

            @pl.when(d != e)
            def _():
                cp_produced(d).start()

            @pl.when(d == e)
            def _():
                fromexp[e] = produced[d]

    waiting = [z]
    for n in range(1, HALF // 2 + 1):
        for j in waiting:
            down(j)
        waiting = []
        for v in range(SUBS // 2):
            for k in (2 * n - 1, 2 * n):
                for way in (1, -1):
                    if k <= reach(v, way):
                        cp_act_in(v, way, k).wait_recv()
                        forward(v, way, k)
                        if v:
                            waiting.append(lax.rem(z - way * k + NZ, NZ))
    for j in waiting:
        down(j)
    drains.append(lambda: loop(1, NE, lambda i: cp_from(i).wait_send()))
    loop(1, NE, lambda i: cp_from(i).wait_recv())
    back = dot(unplace[...], fromexp[...].reshape(NE * 16, 2 * DS)).astype(BF16)
    yrows[...] = back.reshape(8, ROWS, 2 * DS)

    def cp_back(i):
        return remote(yrows.at[i], yback.at[z // 2], s_yb.at[i], r_yb.at[z // 2], 8 * parity + i, e)

    def cp_back_from(i):
        return remote(yrows.at[i], yback.at[i], s_yb.at[i], r_yb.at[i], 2 * i + half, e)

    def sent_back(act_on):
        def one(n):
            odd = lax.rem(n, 2)
            step = odd * ((n + 1) // 2) + (1 - odd) * (8 - n // 2)
            near = jnp.where(half == parity, 12 - step, step)
            i = lax.rem(z // 2 + n, 8)

            @pl.when(8 * parity + i != z)
            def _():
                act_on(i)
        loop(0, 8, one)

    sent_back(lambda i: cp_back(i).start())
    need(gw_ref)
    gw_col = jnp.sum(jnp.where(eye, gw_ref[...], 0.0), axis=1, keepdims=True)
    finish()

    def mix(n):
        i = lax.rem(z // 2 + 8 - n, 8)

        @pl.when(2 * i + half != z)
        def _():
            cp_back_from(i).wait_recv()

        @pl.when(2 * i + half == z)
        def _():
            yback[i] = yrows[lax.rem(z, 8)]

        rows = jnp.concatenate([hidden[2 * i], hidden[2 * i + 1]], axis=1).astype(F32)
        mixed = rows + gw_col * yback[i].astype(F32)
        out_ref[:, pl.ds(pl.multiple_of(i * 2 * DS, 2 * DS), 2 * DS)] = mixed.astype(BF16)

    loop(0, 8, mix)
    sent_back(lambda i: cp_back(i).wait_send())


def shards(q, k, v, log_decay, gain, residual, ids, gate_weights, w_gate, w_up, w_down):
    sem = pltpu.SemaphoreType.DMA
    pair = lambda *shape: [sem(shape), sem(shape)]
    args = (
        q, k, v, log_decay.T, gain.reshape(1, HD), residual, ids.T, gate_weights.T,
        w_gate[0], w_up[0], w_down[0],
    )
    scratch = [
        *[pltpu.VMEM(a.shape, a.dtype) for a in args[:-1]],
        pltpu.VMEM((2, FFE, DS), BF16),
        pltpu.VMEM((NZ, 2, 128), F32),
        pltpu.VMEM((8, 16, HD), BF16),
        pltpu.VMEM((NZ, 16, HD), BF16),
        pltpu.VMEM((NZ, 16, HD), BF16),
        pltpu.VMEM((8, 16, HD), BF16),
        pltpu.VMEM((SEC, HD), F32),
        pltpu.VMEM((SEC, HD), BF16),
        pltpu.VMEM((NE, ROWS, HD), BF16),
        pltpu.VMEM((NZ, ROWS, DS), BF16),
        pltpu.VMEM((NZ, ROWS, DS), BF16),
        pltpu.VMEM((NE * 32, NZ * ROWS), BF16),
        pltpu.VMEM((8 * ROWS, NE * 16), BF16),
        pltpu.VMEM((NE * 32, DS), BF16),
        pltpu.VMEM((NE, 32, DS), BF16),
        pltpu.VMEM((SUBS, CHUNK, WIDE), BF16),
        pltpu.VMEM((SUBS, CHUNK, WIDE), BF16),
        pltpu.VMEM((HALF, SUBS, CHUNK, WIDE), BF16),
        pltpu.VMEM((HALF, SUBS, CHUNK, WIDE), BF16),
        pltpu.VMEM((HALF, SUBS, CHUNK, WIDE), BF16),
        pltpu.VMEM((HALF, SUBS, CHUNK, WIDE), BF16),
        pltpu.VMEM((SUBS // 2, 2, NZ, CHUNK // 2, WIDE), BF16),
        *[pltpu.VMEM((NE, 16, 2 * DS), BF16)] * 2,
        *[pltpu.VMEM((8, ROWS, 2 * DS), BF16)] * 2,
        sem((len(args),)),
        *pair(3),
        *pair(NZ), *pair(NZ), *pair(NZ), *pair(NE), *pair(NZ), *pair(NE),
        *pair(HALF, SUBS), *pair(HALF, SUBS), *pair(SUBS // 2, 2, HALF + 1), *pair(NE), *pair(8),
    ]
    return pl.pallas_call(
        kernel,
        out_shape=jax.ShapeDtypeStruct(residual.shape, BF16),
        in_specs=[pl.BlockSpec(memory_space=pltpu.HBM)] * len(args),
        out_specs=pl.BlockSpec(memory_space=pltpu.VMEM),
        scratch_shapes=scratch,
        name="layer_pair",
        compiler_params=pltpu.CompilerParams(
            collective_id=0, has_side_effects=True, vmem_limit_bytes=54848 << 10
        ),
    )(*args)


def solution(mesh):
    return jax.shard_map(
        shards,
        mesh=mesh,
        in_specs=(
            P("ctx", "exp"),
            P("ctx", "exp"),
            P("ctx", "exp"),
            P("ctx", "exp"),
            P("exp"),
            P(("ctx", "exp"), None),
            P(("ctx", "exp"), None),
            P(("ctx", "exp"), None),
            P("exp", "ctx", None),
            P("exp", "ctx", None),
            P("exp", None, "ctx"),
        ),
        out_specs=P(("ctx", "exp"), None),
        check_vma=False,
    )
```
